128 devices in a mesh: group: 16 (over x_hi, y, core), mp: 8 (over z, x_lo).
Axes of the slice: x: 4 (x_hi: 2, x_lo: 2; x = x_hi * 2 + x_lo), y: 4, z: 4, core: 2. Of those that a mesh axis runs over, the one named last changes fastest.
Arguments:
- tokens: bfloat16 [2, 2048, 8192], P(None, 'group'), may hold values from -6 to 6
- q_weight: bfloat16 [8192, 8192], P('group', 'mp'), may hold values from -0.0625 to 0.0625
- kv_weight: bfloat16 [8192, 2048], P('group', 'mp'), may hold values from -0.0625 to 0.0625
- o_weight: bfloat16 [8192, 8192], P('mp', 'group'), may hold values from -0.5 to 0.5
- kv_pool: bfloat16 [16384, 16, 2048], P('group', None, 'mp'), may hold values from -51 to 51
- send_list: int32 [16, 16, 8], P('group'), may hold values from 0 to 1023
- page_table: int32 [2048, 8], P('group'), may hold values from 0 to 1151
- lengths: int32 [2048], P('group'), may hold values from 1 to 128
Outputs:
- mixed: bfloat16 [2, 2048, 8192], P(None, 'group', 'mp')
The draws below stay inside these ranges and needn't reach their ends.
Inputs may be any that keep to these rules, and one draw needn't show every extreme that they name: `page_table`: entries below 1024 name a page of the group index's own pool; entry 1024 + s * 8 + c names the page that source s sends in slot c. `send_list`: page ids of the sending group index's own pool; a page may be named more than once.
All inputs are finite; a program needn't handle non-finite values.
Results may differ from the reference program's by a relative error of at most 0.018.
Values may be sent and summed in bfloat16 or wider, within the bound.
A program may use at most 192 MiB of HBM per device.

```python
import jax
import jax.numpy as jnp
from jax import lax

D = 8192
HQ = 64
KVH = 8
HD = 128
PAGE = 16
MAXP = 8
ROW_DEV = 128
POOL = 1024
CAP = 8
ROWS = 2048
POOL_ALL = 16384
SLOTS = 1152
N_GROUP = 16
N_MP = 8


def draw_kv_pool(key, part):
    key = jax.random.fold_in(key, 11)
    first = jax.random.fold_in(key, 0)
    shape = (POOL_ALL, PAGE, KVH * 2 * HD)
    values = jnp.clip(jax.random.normal(first, shape, jnp.float32), -6.0, 6.0)
    return values.astype(jnp.bfloat16)


def set_ends(array, key, low, largest):
    longest = array.shape.index(max(array.shape))
    spots = []
    for shift in (0, 1):
        where = [jax.random.randint(jax.random.fold_in(key, axis), (), 0, length) for axis, length in enumerate(array.shape)]
        where[longest] = (where[longest] + shift) % array.shape[longest]
        spots.append(tuple(where))
    return array.at[spots[0]].set(low).at[spots[1]].set(largest)


def shard_levels(own_key, shape, cuts, least, top_value):
    def one(dim, parts):
        heights = jax.random.uniform(jax.random.fold_in(jax.random.fold_in(own_key, 6), dim), (parts,), jnp.float32, least / len(cuts), top_value / len(cuts))
        return jnp.repeat(jnp.exp(heights), shape[dim] // parts).reshape((-1,) + (1,) * (len(shape) - dim - 1))

    gain = one(*cuts[0])
    for cut in cuts[1:]:
        gain = gain * one(*cut)
    return gain


def centred(rng, shape, scale, reach, cuts=(), kind=jnp.bfloat16):
    entries = scale * jax.random.normal(rng, shape, jnp.float32)
    if cuts:
        entries = entries * shard_levels(rng, shape, cuts, -0.22, 0.18)
    return jnp.clip(entries, -reach, reach).astype(kind)


def setup_inputs(seed: int = 0) -> dict:
    seeds = jax.random.split(jax.random.key(seed), 9)
    tokens = centred(seeds[0], (2, ROWS, D), 1.0, 6.0, ((1, 16),))
    q_weight = centred(seeds[1], (D, HQ * HD), D ** -0.5, 0.0625, ((0, 16), (1, 8)))
    kv_weight = centred(seeds[2], (D, KVH * 2 * HD), D ** -0.5, 0.0625, ((0, 16), (1, 8)))
    o_weight = centred(seeds[3], (HQ * HD, D), (HQ * HD // 64) ** -0.5, 0.5, ((0, 8), (1, 16)))
    kv_pool = draw_kv_pool(jax.random.fold_in(seeds[8], 71), 0)
    send_list = set_ends(jax.random.randint(seeds[5], (N_GROUP, N_GROUP, CAP), 0, POOL), jax.random.fold_in(seeds[5], 1), 0, POOL - 1).astype(jnp.int32)
    page_table = set_ends(jax.random.randint(seeds[6], (ROWS, MAXP), 0, SLOTS), jax.random.fold_in(seeds[6], 1), 0, SLOTS - 1).astype(jnp.int32)
    lengths = set_ends(jax.random.randint(seeds[7], (ROWS,), 1, MAXP * PAGE + 1), jax.random.fold_in(seeds[7], 1), 1, MAXP * PAGE).astype(jnp.int32)
    return {"tokens": tokens, "q_weight": q_weight, "kv_weight": kv_weight, "o_weight": o_weight, "kv_pool": kv_pool, "send_list": send_list, "page_table": page_table, "lengths": lengths}


def stored(value):
    return lax.optimization_barrier(value.astype(jnp.bfloat16)).astype(jnp.float32)


def rotate(values, position):
    half = values.shape[-1] // 2
    inverse = 500000.0 ** (-(jnp.arange(half, dtype=jnp.float32) * 2.0) / (2.0 * half))
    angle = position[..., None] * inverse
    cosine = jnp.cos(angle)
    sine = jnp.sin(angle)
    first = values[..., :half]
    second = values[..., half:]
    return jnp.concatenate([first * cosine - second * sine, second * cosine + first * sine], axis=-1)


def attend(held, table, query, key_new, value_new, length):
    rows = table.shape[0]
    cache = held[table].reshape(rows, MAXP * PAGE, KVH, 2, HD)
    key_cache = cache[:, :, :, 0].astype(jnp.float32)
    value_cache = cache[:, :, :, 1].astype(jnp.float32)
    grouped = query.astype(jnp.float32).reshape(2, rows, KVH, HQ // KVH, HD)
    scale = 1.0 / (HD ** 0.5)
    score_cache = jnp.einsum("trkgd,rckd->trkgc", grouped, key_cache) * scale
    live = jnp.arange(MAXP * PAGE)[None, :] < length[:, None]
    score_cache = jnp.where(live[None, :, None, None, :], score_cache, -jnp.inf)
    score_new = jnp.einsum("trkgd,urkd->trkgu", grouped, key_new.astype(jnp.float32)) * scale
    causal = jnp.arange(2)[:, None] >= jnp.arange(2)[None, :]
    score_new = jnp.where(causal[:, None, None, None, :], score_new, -jnp.inf)
    top = jnp.maximum(jnp.max(score_cache, axis=-1), jnp.max(score_new, axis=-1))
    exp_cache = jnp.exp(score_cache - top[..., None])
    exp_new = jnp.exp(score_new - top[..., None])
    total = jnp.sum(exp_cache, axis=-1) + jnp.sum(exp_new, axis=-1)
    numer = jnp.einsum("trkgc,rckd->trkgd", stored(exp_cache), value_cache)
    numer = numer + jnp.einsum("trkgu,urkd->trkgd", stored(exp_new), value_new.astype(jnp.float32))
    return (numer / total[..., None]).reshape(2, rows, HQ * HD).astype(jnp.bfloat16)


def reference(tokens, q_weight, kv_weight, o_weight, kv_pool, send_list, page_table, lengths):
    flat = tokens.reshape(2 * ROWS, D)
    query = jnp.dot(flat, q_weight, preferred_element_type=jnp.float32).reshape(2, ROWS, HQ, HD)
    keyval = jnp.dot(flat, kv_weight, preferred_element_type=jnp.float32).reshape(2, ROWS, KVH, 2, HD)
    position = lengths[None, :].astype(jnp.float32) + jnp.arange(2, dtype=jnp.float32)[:, None]
    query = rotate(query, position[:, :, None]).astype(jnp.bfloat16)
    key_new = rotate(keyval[:, :, :, 0], position[:, :, None]).astype(jnp.bfloat16)
    value_new = keyval[:, :, :, 1].astype(jnp.bfloat16)
    width = KVH * 2 * HD
    pools = kv_pool.reshape(N_GROUP, POOL, PAGE, width)
    moved = pools[jnp.arange(N_GROUP)[:, None, None], send_list]
    moved = jnp.transpose(moved, (1, 0, 2, 3, 4)).reshape(N_GROUP, N_GROUP * CAP, PAGE, width)
    held = jnp.concatenate([pools, moved], axis=1)

    def per_group(items):
        group_held, table, group_query, group_key, group_value, length = items
        return attend(group_held, table, group_query, group_key, group_value, length)

    def lead(values):
        return jnp.swapaxes(values.reshape((2, N_GROUP, ROW_DEV) + values.shape[2:]), 0, 1)

    attn = lax.map(per_group, (held, page_table.reshape(N_GROUP, ROW_DEV, MAXP), lead(query), lead(key_new), lead(value_new), lengths.reshape(N_GROUP, ROW_DEV)))
    attn = jnp.swapaxes(attn, 0, 1).reshape(2 * ROWS, HQ * HD)
    block = HQ * HD // N_MP
    mixed = jnp.zeros((2 * ROWS, D), jnp.float32)
    for index in range(N_MP):
        part_term = jnp.dot(attn[:, index * block:(index + 1) * block], o_weight[index * block:(index + 1) * block], preferred_element_type=jnp.float32)
        mixed = mixed + stored(part_term)
    return mixed.astype(jnp.bfloat16).reshape(2, ROWS, D)
```

```python
import jax
import jax.numpy as jnp
from jax import lax
from jax.experimental import pallas as pl
from jax.experimental.pallas import tpu as pltpu
from jax.sharding import PartitionSpec as P

HD = 128
MESH = pl.DeviceIdType.MESH
BF16 = jnp.bfloat16
F32 = jnp.float32

Q_UP, Q_DN, Q_FUP, Q_FDN, Q_SIB = 0, 2, 4, 5, 6
T_X, T_Z, P_X = 11, 12, 15
O_X, O_UP, O_DN, O_FUP, O_FDN, O_SIB = 16, 17, 21, 25, 27, 29
R_X = 39
N_REMOTE = 40


def kernel(
    tokens, q_weight, kv_weight, o_weight, pool, cos, sin, send_list, table, lengths, out,
    wq, wo, tok, held, arrived, outgoing, acc, psend, precv, q3, k_new, v_new, attn,
    part, zrecv, xsend, xrecv,
    ssem, rsem, page_ssem, page_rsem, z_ssem, z_rsem, lsem,
):
    g = lax.axis_index("group")
    m = lax.axis_index("mp")
    xh, y, c = g // 8, (g // 2) % 4, g % 2
    z, xl = m // 2, m % 2
    up, dn, opp = (y + 1) % 4, (y + 3) % 4, (y + 2) % 4

    def in_group(xh_, y_, c_):
        return (xh_ * 8 + y_ * 2 + c_, m)

    to_up, to_dn = in_group(xh, up, c), in_group(xh, dn, c)
    to_x, to_sib = in_group(1 - xh, y, c), in_group(xh, y, 1 - c)

    def remote(src, dst, number, device):
        return pltpu.make_async_remote_copy(
            src_ref=src, dst_ref=dst, send_sem=ssem.at[number], recv_sem=rsem.at[number],
            device_id=device, device_id_type=MESH,
        )

    half = pl.multiple_of(xh * 4096, 4096)
    other_half = pl.multiple_of((1 - xh) * 4096, 4096)
    my_rows = pl.ds(pl.multiple_of(c * 512, 512), 512)
    my_cols = pl.ds(pl.multiple_of(c * 512, 512), 512)
    own_chip = xh * 4 + y
    loads = [
        pltpu.make_async_copy(q_weight, wq.at[y, my_rows, pl.ds(0, 1024)], lsem.at[0]),
        pltpu.make_async_copy(kv_weight, wq.at[y, my_rows, pl.ds(1024, 256)], lsem.at[1]),
        pltpu.make_async_copy(o_weight, wo.at[own_chip, :, my_cols], lsem.at[2]),
        pltpu.make_async_copy(pool, held.at[pl.ds(0, 1024)], lsem.at[3]),
        pltpu.make_async_copy(tokens.at[:, pl.ds(half, 4096)], tok.at[0], lsem.at[4]),
    ]
    for load in loads:
        load.start()

    barrier = pltpu.get_barrier_semaphore()
    for off in range(1, 16):
        pl.semaphore_signal(barrier, inc=1, device_id=((g + off) % 16, m), device_id_type=MESH)
    for off in range(1, 4):
        pl.semaphore_signal(
            barrier, inc=1, device_id=(g, ((z + off) % 4) * 2 + xl), device_id_type=MESH
        )
    to_lo = (g, z * 2 + 1 - xl)
    pl.semaphore_signal(barrier, inc=1, device_id=to_lo, device_id_type=MESH)
    pl.semaphore_wait(barrier, 19)

    sent = []

    def start(copy):
        copy.start()
        sent.append(copy)
        return copy

    my_quarter = pl.ds(pl.multiple_of(z * 64, 64), 64)
    t_x = start(remote(
        tokens.at[my_quarter, pl.ds(other_half, 4096)], tok.at[1, my_quarter], T_X, to_x))

    def q_piece(yy, h):
        return wq.at[yy, pl.ds(pl.multiple_of(c * 512 + h * 256, 256), 256)]

    def q_block(yy):
        return wq.at[yy, my_rows]

    loads[0].wait()
    loads[1].wait()
    q_up, q_dn = [None, None], [None, None]
    for h in (0, 1):
        q_up[h] = start(remote(q_piece(y, h), q_piece(y, h), Q_UP + h, to_up))
        q_dn[1 - h] = start(remote(q_piece(y, 1 - h), q_piece(y, 1 - h), Q_DN + 1 - h, to_dn))
    q_sib = [start(remote(q_block(y), q_block(y), Q_SIB, to_sib))]

    def o_block(chip):
        return wo.at[chip, :, my_cols]

    def o_piece(chip, h):
        return wo.at[chip, pl.ds(h * 512, 512), my_cols]

    loads[2].wait()
    o_x = start(remote(o_block(own_chip), o_block(own_chip), O_X, to_x))
    o_sib = [start(remote(o_block(own_chip), o_block(own_chip), O_SIB, to_sib))]

    loads[3].wait()

    def gather_page(i, carry):
        outgoing[i] = held[send_list[i]]
        return carry

    lax.fori_loop(0, 128, gather_page, 0)

    t_x.wait_recv()
    t_z = []
    for off in range(1, 4):
        t_z.append(start(remote(
            tok.at[1, my_quarter], tok.at[1, my_quarter], T_Z + off - 1,
            (g, ((z + off) % 4) * 2 + xl))))

    def project(which, yy, first):
        left = pl.ds(pl.multiple_of(yy * 1024, 1024), 1024)

        def step(n, carry):
            cols = pl.ds(pl.multiple_of(n * 256, 256), 256)
            product = jnp.dot(
                tok[which, :, left], wq[yy, :, cols], preferred_element_type=F32)
            acc[which, :, cols] = product if first else acc[which, :, cols] + product
            return carry

        lax.fori_loop(0, 5, step, 0)

    q_up[0].wait_recv()
    q_fup = start(remote(q_piece(dn, 0), q_piece(dn, 0), Q_FUP, to_up))
    q_dn[1].wait_recv()
    q_fdn = start(remote(q_piece(up, 1), q_piece(up, 1), Q_FDN, to_dn))

    loads[4].wait()
    q_sib[0].wait_recv()
    project(0, y, True)

    q_up[1].wait_recv()
    q_sib.append(start(remote(q_block(dn), q_block(dn), Q_SIB + 1, to_sib)))
    q_dn[0].wait_recv()
    q_sib.append(start(remote(q_block(up), q_block(up), Q_SIB + 2, to_sib)))
    q_sib[1].wait_recv()
    project(0, dn, False)
    q_sib[2].wait_recv()
    project(0, up, False)

    for copy in t_z:
        copy.wait_recv()
    project(1, y, True)
    project(1, dn, False)
    project(1, up, False)

    q_fup.wait_recv()
    q_sib.append(start(remote(q_piece(opp, 0), q_piece(opp, 0), Q_SIB + 3, to_sib)))
    q_fdn.wait_recv()
    q_sib.append(start(remote(q_piece(opp, 1), q_piece(opp, 1), Q_SIB + 4, to_sib)))

    pages = []
    for off in range(1, 16):
        there = (g + off) % 16
        copy = pltpu.make_async_remote_copy(
            src_ref=outgoing.at[pl.ds(there * 8, 8)], dst_ref=arrived.at[pl.ds(g * 8, 8)],
            send_sem=page_ssem.at[off - 1], recv_sem=page_rsem.at[off - 1],
            device_id=(there, m), device_id_type=MESH)
        copy.start()
        pages.append(copy)
        sent.append(copy)
    own_pages = pltpu.make_async_copy(
        outgoing.at[pl.ds(g * 8, 8)], arrived.at[pl.ds(g * 8, 8)], lsem.at[5])
    own_pages.start()

    o_x.wait_recv()
    partner_chip = (1 - xh) * 4 + y
    o_sib.append(start(remote(o_block(partner_chip), o_block(partner_chip), O_SIB + 1, to_sib)))
    o_up, o_dn = [[None, None], [None, None]], [[None, None], [None, None]]
    for k, chip in enumerate((own_chip, partner_chip)):
        for h in (0, 1):
            o_up[k][h] = start(remote(
                o_piece(chip, h), o_piece(chip, h), O_UP + 2 * k + h, to_up))
            o_dn[k][1 - h] = start(remote(
                o_piece(chip, 1 - h), o_piece(chip, 1 - h), O_DN + 2 * k + 1 - h, to_dn))

    q_sib[3].wait_recv()
    q_sib[4].wait_recv()
    project(1, opp, False)
    psend[...] = acc[1].astype(BF16)
    p_x = start(remote(psend, precv, P_X, to_x))
    project(0, opp, False)

    for copy in pages:
        copy.wait_recv()
    own_pages.wait()
    append = pltpu.make_async_copy(arrived, held.at[pl.ds(1024, 128)], lsem.at[6])
    append.start()

    p_x.wait_recv()
    for t in range(2):
        rows = pl.ds(t * 128, 128)

        def whole(first):
            cols = pl.ds(first, HD)
            return acc[0, rows, cols] + precv[rows, cols].astype(F32)

        def rotated(value):
            turned = jnp.concatenate([value[:, 64:], value[:, :64]], axis=1)
            value = value * cos[rows, :] + turned * sin[rows, :]
            return value.astype(BF16).astype(F32)

        for h in range(8):
            q3[:, t * 8 + h, :] = rotated(whole(h * HD))
        k_new[rows, :] = rotated(whole(1024))
        v_new[rows, :] = whole(1024 + HD).astype(BF16).astype(F32)
    append.wait()

    scale = 1.0 / HD**0.5
    position = lax.broadcasted_iota(jnp.int32, (16, 128), 1)
    second = lax.broadcasted_iota(jnp.int32, (16, 1), 0) >= 8

    def attend(i, carry):
        for k in range(8):
            r = i * 8 + k
            cache = jnp.concatenate([held[table[r * 8 + j]] for j in range(8)], axis=0)
            query = q3[r]
            scores = lax.dot_general(
                query.astype(BF16), cache[:, :HD], (((1,), (1,)), ((), ())),
                preferred_element_type=F32) * scale
            scores = jnp.where(position < lengths[r], scores, -jnp.inf)
            new0 = jnp.sum(query * k_new[pl.ds(r, 1), :], axis=1, keepdims=True) * scale
            new1 = jnp.sum(query * k_new[pl.ds(128 + r, 1), :], axis=1, keepdims=True) * scale
            new1 = jnp.where(second, new1, -jnp.inf)
            top = jnp.maximum(
                jnp.max(scores, axis=1, keepdims=True), jnp.maximum(new0, new1))
            weights = jnp.exp(scores - top)
            weight0 = jnp.exp(new0 - top)
            weight1 = jnp.exp(new1 - top)
            total = jnp.sum(weights, axis=1, keepdims=True) + weight0 + weight1
            numer = jnp.dot(
                weights.astype(BF16), cache[:, HD:], preferred_element_type=F32)
            numer = numer + weight0.astype(BF16).astype(F32) * v_new[pl.ds(r, 1), :]
            numer = numer + weight1.astype(BF16).astype(F32) * v_new[pl.ds(128 + r, 1), :]
            q3[r] = numer / total
        return carry

    lax.fori_loop(0, 16, attend, 0)
    for t in range(2):
        for h in range(8):
            attn[pl.ds(t * 128, 128), pl.ds(h * HD, HD)] = q3[:, t * 8 + h, :].astype(BF16)

    def z_copy(chip):
        there = chip // 2
        slot = (z - there + 4) % 4 - 1
        return pltpu.make_async_remote_copy(
            src_ref=part.at[chip], dst_ref=zrecv.at[slot, chip % 2],
            send_sem=z_ssem.at[chip], recv_sem=z_rsem.at[slot, chip % 2],
            device_id=(g, there * 2 + xl), device_id_type=MESH)

    def unit(chip):
        def step(n, carry):
            cols = pl.ds(pl.multiple_of(n * 256, 256), 256)
            part[chip, :, cols] = jnp.dot(
                attn[...], wo[chip, :, cols], preferred_element_type=F32).astype(BF16)
            return carry

        lax.fori_loop(0, 4, step, 0)

        @pl.when(chip // 2 != z)
        def _():
            z_copy(chip).start()

    o_sib[0].wait_recv()
    unit(own_chip)
    o_sib[1].wait_recv()
    unit(partner_chip)
    o_fup, o_fdn = [], []
    for k, side in enumerate((xh, 1 - xh)):
        o_up[k][0].wait_recv()
        o_fup.append(start(remote(
            o_piece(side * 4 + dn, 0), o_piece(side * 4 + dn, 0), O_FUP + k, to_up)))
        o_dn[k][1].wait_recv()
        o_fdn.append(start(remote(
            o_piece(side * 4 + up, 1), o_piece(side * 4 + up, 1), O_FDN + k, to_dn)))
        o_up[k][1].wait_recv()
        o_sib.append(start(remote(
            o_block(side * 4 + dn), o_block(side * 4 + dn), O_SIB + 2 + 2 * k, to_sib)))
        o_dn[k][0].wait_recv()
        o_sib.append(start(remote(
            o_block(side * 4 + up), o_block(side * 4 + up), O_SIB + 3 + 2 * k, to_sib)))
        o_sib[2 + 2 * k].wait_recv()
        unit(side * 4 + dn)
        o_sib[3 + 2 * k].wait_recv()
        unit(side * 4 + up)
    for k, side in enumerate((xh, 1 - xh)):
        o_fup[k].wait_recv()
        o_sib.append(start(remote(
            o_piece(side * 4 + opp, 0), o_piece(side * 4 + opp, 0), O_SIB + 6 + 2 * k, to_sib)))
        o_fdn[k].wait_recv()
        o_sib.append(start(remote(
            o_piece(side * 4 + opp, 1), o_piece(side * 4 + opp, 1), O_SIB + 7 + 2 * k, to_sib)))
        o_sib[6 + 2 * k].wait_recv()
        o_sib[7 + 2 * k].wait_recv()
        unit(side * 4 + opp)

    def z_sum(lo, cols):
        total = part[z * 2 + lo, :, cols].astype(F32)
        for slot in range(3):
            total = total + zrecv[slot, lo, :, cols].astype(F32)
        return total

    def z_wait(lo):
        for slot in range(3):
            pltpu.make_async_copy(
                zrecv.at[slot, lo], zrecv.at[slot, lo], z_rsem.at[slot, lo]).wait()

    z_wait(1 - xl)

    def sum_other(n, carry):
        cols = pl.ds(pl.multiple_of(n * 256, 256), 256)
        xsend[:, cols] = z_sum(1 - xl, cols).astype(BF16)
        return carry

    lax.fori_loop(0, 4, sum_other, 0)
    r_x = start(remote(xsend, xrecv, R_X, to_lo))
    z_wait(xl)
    r_x.wait_recv()

    def sum_own(n, carry):
        cols = pl.ds(pl.multiple_of(n * 256, 256), 256)
        out[:, cols] = (z_sum(xl, cols) + xrecv[:, cols].astype(F32)).astype(BF16)
        return carry

    lax.fori_loop(0, 4, sum_own, 0)

    for copy in sent:
        copy.wait_send()
    for chip in range(8):
        @pl.when(chip // 2 != z)
        def _():
            z_copy(chip).wait_send()


def per_device(tokens, q_weight, kv_weight, o_weight, kv_pool, send_list, page_table, lengths):
    rows = tokens.shape[1]
    flat = tokens.reshape(2 * rows, tokens.shape[2])
    inverse = 500000.0 ** (-(jnp.arange(64, dtype=F32) * 2.0) / 128.0)
    position = (lengths[None, :].astype(F32) + jnp.arange(2, dtype=F32)[:, None]).reshape(-1)
    angle = position[:, None] * inverse
    cosine, sine = jnp.cos(angle), jnp.sin(angle)
    cos = jnp.concatenate([cosine, cosine], axis=1)
    sin = jnp.concatenate([-sine, sine], axis=1)
    hbm = pl.BlockSpec(memory_space=pl.ANY)
    vmem = pl.BlockSpec(memory_space=pltpu.VMEM)
    smem = pl.BlockSpec(memory_space=pltpu.SMEM)
    mixed = pl.pallas_call(
        kernel,
        out_shape=jax.ShapeDtypeStruct((256, 1024), BF16),
        in_specs=[hbm] * 5 + [vmem] * 2 + [smem] * 3,
        out_specs=vmem,
        scratch_shapes=[
            pltpu.VMEM((4, 1024, 1280), BF16),
            pltpu.VMEM((8, 1024, 1024), BF16),
            pltpu.VMEM((2, 256, 4096), BF16),
            pltpu.VMEM((1152, 16, 256), BF16),
            pltpu.VMEM((128, 16, 256), BF16),
            pltpu.VMEM((128, 16, 256), BF16),
            pltpu.VMEM((2, 256, 1280), F32),
            pltpu.VMEM((256, 1280), BF16),
            pltpu.VMEM((256, 1280), BF16),
            pltpu.VMEM((128, 16, 128), F32),
            pltpu.VMEM((256, 128), F32),
            pltpu.VMEM((256, 128), F32),
            pltpu.VMEM((256, 1024), BF16),
            pltpu.VMEM((8, 256, 1024), BF16),
            pltpu.VMEM((3, 2, 256, 1024), BF16),
            pltpu.VMEM((256, 1024), BF16),
            pltpu.VMEM((256, 1024), BF16),
            pltpu.SemaphoreType.DMA((N_REMOTE,)),
            pltpu.SemaphoreType.DMA((N_REMOTE,)),
            pltpu.SemaphoreType.DMA((15,)),
            pltpu.SemaphoreType.DMA((15,)),
            pltpu.SemaphoreType.DMA((8,)),
            pltpu.SemaphoreType.DMA((3, 2)),
            pltpu.SemaphoreType.DMA((7,)),
        ],
        compiler_params=pltpu.CompilerParams(
            collective_id=0, has_side_effects=True, vmem_limit_bytes=60 * 2**20),
    )(
        flat, q_weight, kv_weight, o_weight, kv_pool, cos, sin,
        send_list.reshape(-1), page_table.reshape(-1), lengths,
    )
    return mixed.reshape(2, rows, -1)


def solution(mesh):
    in_specs = (
        P(None, "group", None),
        P("group", "mp"),
        P("group", "mp"),
        P("mp", "group"),
        P("group", None, "mp"),
        P("group", None, None),
        P("group", None),
        P("group"),
    )
    out_specs = P(None, "group", "mp")
    return jax.shard_map(
        per_device, mesh=mesh, in_specs=in_specs, out_specs=out_specs, check_vma=False
    )
```

```python
import jax
import jax.numpy as jnp
from jax import lax
from jax.experimental import pallas as pl
from jax.experimental.pallas import tpu as pltpu
from jax.sharding import PartitionSpec as P

HD = 128
GROUP = 16
MESH = pl.DeviceIdType.MESH
BF16 = jnp.bfloat16
F32 = jnp.float32
LOG_BASE = 13.122363377404328

Q_UP, Q_DN, Q_FUP, Q_FDN, Q_SIB = 0, 2, 4, 5, 6
T_X, T_Z, P_X, G_X, G_Y = 11, 12, 15, 16, 17
B_UP, B_DN, B_FUP, B_FDN, B_X, B_SIB = 24, 26, 28, 29, 30, 35
A_X, A_UP, A_DN, A_FUP, A_FDN, A_SIB = 45, 46, 50, 54, 56, 58
R_X = 68
N_REMOTE = 82
WIDTH = (768, 512)


def kernel(
    tokens, q_weight, kv_weight, o_weight, pool, row_lengths, send_list, table, lengths, out,
    wq0, wq1, wo, tok, held, arrived, leaving, staying, acc0, acc1, psend0, psend1, precv0, precv1, q3, k_new, v_new, attn,
    part, zmid, zrecv, xsend, xrecv,
    ssem, rsem, z_ssem, mid_rsem, z_rsem, lsem,
):
    g = lax.axis_index("group")
    m = lax.axis_index("mp")
    wq, acc, psend, precv = (wq0, wq1), (acc0, acc1), (psend0, psend1), (precv0, precv1)
    xh, y, c = g // 8, (g // 2) % 4, g % 2
    z, xl = m // 2, m % 2
    up, dn, opp = (y + 1) % 4, (y + 3) % 4, (y + 2) % 4
    z_up, z_dn = (z + 1) % 4, (z + 3) % 4
    me = y * 2 + c

    def in_group(xh_, y_, c_):
        return (xh_ * 8 + y_ * 2 + c_, m)

    to_up, to_dn = in_group(xh, up, c), in_group(xh, dn, c)
    to_x, to_sib = in_group(1 - xh, y, c), in_group(xh, y, 1 - c)
    to_lo = (g, z * 2 + 1 - xl)

    def at_z(z_):
        return (g, z_ * 2 + xl)

    half = pl.multiple_of(xh * 4096, 4096)
    other_half = pl.multiple_of((1 - xh) * 4096, 4096)
    my_rows = pl.ds(pl.multiple_of(c * 512, 512), 512)
    my_cols = pl.ds(pl.multiple_of(c * 256, 256), 256)
    own_chip, partner_chip = xh * 4 + y, (1 - xh) * 4 + y
    loads = [
        pltpu.make_async_copy(kv_weight, wq0.at[y, my_rows, pl.ds(0, 256)], lsem.at[0]),
        pltpu.make_async_copy(
            q_weight.at[:, pl.ds(0, 512)], wq0.at[y, my_rows, pl.ds(256, 512)], lsem.at[1]),
        pltpu.make_async_copy(q_weight.at[:, pl.ds(512, 512)], wq1.at[y, my_rows], lsem.at[9]),
        pltpu.make_async_copy(pool, held.at[pl.ds(0, 1024)], lsem.at[2]),
        pltpu.make_async_copy(
            o_weight.at[:, pl.ds(256, 256)], wo.at[1, own_chip, :, my_cols], lsem.at[3]),
        pltpu.make_async_copy(
            o_weight.at[:, pl.ds(0, 256)], wo.at[0, own_chip, :, my_cols], lsem.at[4]),
        pltpu.make_async_copy(tokens.at[:, pl.ds(half, 4096)], tok.at[0], lsem.at[5]),
    ]
    for load in loads:
        load.start()

    barrier = pltpu.get_barrier_semaphore()
    for off in range(1, 8):
        pl.semaphore_signal(
            barrier, inc=1, device_id=(xh * 8 + (me + off) % 8, m), device_id_type=MESH)
    for off in range(1, 4):
        pl.semaphore_signal(barrier, inc=1, device_id=at_z((z + off) % 4), device_id_type=MESH)
    pl.semaphore_signal(barrier, inc=1, device_id=to_x, device_id_type=MESH)
    pl.semaphore_signal(barrier, inc=1, device_id=to_lo, device_id_type=MESH)
    pl.semaphore_wait(barrier, 12)

    sent = []

    def send(ref, number, device, there=None):
        copy = pltpu.make_async_remote_copy(
            src_ref=ref, dst_ref=ref if there is None else there,
            send_sem=ssem.at[number], recv_sem=rsem.at[number],
            device_id=device, device_id_type=MESH,
        )
        copy.start()
        sent.append(copy)
        return copy

    my_quarter = pl.ds(pl.multiple_of(z * 64, 64), 64)
    t_x = send(
        tokens.at[my_quarter, pl.ds(other_half, 4096)], T_X, to_x, tok.at[1, my_quarter])

    def q_piece(part, yy, h):
        return wq[part].at[yy, pl.ds(pl.multiple_of(c * 512 + h * 256, 256), 256)]

    def q_block(part, yy):
        return wq[part].at[yy, my_rows]

    q_up, q_dn, q_sib = [[None, None], [None, None]], [[None, None], [None, None]], [[], []]

    def q_send(part):
        for h in (0, 1):
            q_up[part][h] = send(q_piece(part, y, h), 70 * part + Q_UP + h, to_up)
            q_dn[part][1 - h] = send(q_piece(part, y, 1 - h), 70 * part + Q_DN + 1 - h, to_dn)
        q_sib[part].append(send(q_block(part, y), 70 * part + Q_SIB, to_sib))

    q_fup, q_fdn = [None, None], [None, None]

    def q_forward(part):
        q_up[part][0].wait_recv()
        q_fup[part] = send(q_piece(part, dn, 0), 70 * part + Q_FUP, to_up)
        q_dn[part][1].wait_recv()
        q_fdn[part] = send(q_piece(part, up, 1), 70 * part + Q_FDN, to_dn)

    def q_near(part):
        q_up[part][1].wait_recv()
        q_sib[part].append(send(q_block(part, dn), 70 * part + Q_SIB + 1, to_sib))
        q_dn[part][0].wait_recv()
        q_sib[part].append(send(q_block(part, up), 70 * part + Q_SIB + 2, to_sib))

    def q_far(part):
        q_fup[part].wait_recv()
        q_sib[part].append(send(q_piece(part, opp, 0), 70 * part + Q_SIB + 3, to_sib))
        q_fdn[part].wait_recv()
        q_sib[part].append(send(q_piece(part, opp, 1), 70 * part + Q_SIB + 4, to_sib))

    loads[0].wait()
    loads[1].wait()
    q_send(0)

    loads[3].wait()

    def gather_pages(i, carry):
        for k in range(8):
            leaving[i * 8 + k] = held[send_list[0, (1 - xh) * 8 + i, k]]
            staying[xh, i * 8 + k] = held[send_list[0, xh * 8 + i, k]]
        return carry

    lax.fori_loop(0, 8, gather_pages, 0)

    t_x.wait_recv()
    t_z = []
    for off in range(1, 4):
        t_z.append(send(tok.at[1, my_quarter], T_Z + off - 1, at_z((z + off) % 4)))

    g_x = send(leaving, G_X, to_x, staying.at[xh])

    def o_block(r, chip):
        return wo.at[r, chip, :, my_cols]

    def o_piece(r, chip, h):
        return wo.at[r, chip, pl.ds(h * 512, 512), my_cols]

    q_forward(0)
    loads[2].wait()
    q_send(1)
    loads[4].wait()
    loads[5].wait()
    a_x = send(o_block(1, own_chip), A_X, to_x)
    b_x = [send(o_block(0, own_chip), B_X, to_x)]
    a_sib = [send(o_block(1, own_chip), A_SIB, to_sib)]
    b_sib = [send(o_block(0, own_chip), B_SIB, to_sib)]

    def project(part, which, yy, first=False):
        left = pl.ds(pl.multiple_of(yy * 1024, 1024), 1024)

        def step(n, carry):
            cols = pl.ds(pl.multiple_of(n * 256, 256), 256)
            product = jnp.dot(
                tok[which, :, left], wq[part][yy, :, cols], preferred_element_type=F32)
            acc[part][which, :, cols] = (
                product if first else acc[part][which, :, cols] + product)
            return carry

        lax.fori_loop(0, WIDTH[part] // 256, step, 0)

    loads[6].wait()
    q_sib[0][0].wait_recv()
    project(0, 0, y, True)
    q_near(0)
    q_sib[0][1].wait_recv()
    project(0, 0, dn)
    q_sib[0][2].wait_recv()
    project(0, 0, up)
    q_forward(1)
    q_far(0)

    for copy in t_z:
        copy.wait_recv()
    project(0, 1, y, True)
    project(0, 1, dn)
    project(0, 1, up)
    q_sib[0][3].wait_recv()
    q_sib[0][4].wait_recv()
    project(0, 1, opp)
    psend0[...] = acc0[1].astype(BF16)
    p_x = [send(psend0, P_X, to_x, precv0)]

    q_near(1)
    q_sib[1][0].wait_recv()
    project(1, 1, y, True)
    project(1, 0, y, True)
    q_sib[1][1].wait_recv()
    project(1, 1, dn)
    q_sib[1][2].wait_recv()
    project(1, 1, up)
    q_far(1)

    g_x.wait_recv()
    g_y = []
    my_slot = pl.ds(pl.multiple_of(me * 8, 8), 8)
    for off in range(1, 8):
        there = (me + off) % 8
        slot = pl.ds(pl.multiple_of(there * 8, 8), 8)
        g_y.append(send(
            staying.at[:, slot], G_Y + off - 1, (xh * 8 + there, m), arrived.at[:, my_slot]))
    own_pages = pltpu.make_async_copy(
        staying.at[:, my_slot], arrived.at[:, my_slot], lsem.at[6])
    own_pages.start()
    b_up, b_dn = [None, None], [None, None]
    for h in (0, 1):
        b_up[h] = send(o_piece(0, own_chip, h), B_UP + h, to_up)
        b_dn[1 - h] = send(o_piece(0, own_chip, 1 - h), B_DN + 1 - h, to_dn)

    q_sib[1][3].wait_recv()
    q_sib[1][4].wait_recv()
    project(1, 1, opp)
    psend1[...] = acc1[1].astype(BF16)
    p_x.append(send(psend1, P_X + 66, to_x, precv1))
    project(0, 0, opp)
    project(1, 0, dn)
    project(1, 0, up)
    project(1, 0, opp)

    a_x.wait_recv()
    a_sib.append(send(o_block(1, partner_chip), A_SIB + 1, to_sib))
    b_x[0].wait_recv()
    b_sib.append(send(o_block(0, partner_chip), B_SIB + 1, to_sib))

    diagonal = (
        lax.broadcasted_iota(jnp.int32, (128, 128), 0)
        == lax.broadcasted_iota(jnp.int32, (128, 128), 1))
    lane = lax.broadcasted_iota(jnp.int32, (1, 128), 1)
    inverse = jnp.exp((lane % 64).astype(F32) * (-2.0 / 128.0 * LOG_BASE))
    position = jnp.sum(
        jnp.where(diagonal, row_lengths[...].astype(F32), 0.0), axis=1, keepdims=True)
    tables = []
    for t in range(2):
        angle = (position + float(t)) * inverse
        tables.append((jnp.cos(angle), jnp.where(lane < 64, -1.0, 1.0) * jnp.sin(angle)))

    for copy in g_y:
        copy.wait_recv()
    own_pages.wait()
    append = [
        pltpu.make_async_copy(
            arrived.at[k], held.at[pl.ds(1024 + 64 * k, 64)], lsem.at[7 + k])
        for k in range(2)
    ]
    for copy in append:
        copy.start()

    b_up[0].wait_recv()
    b_fup = send(o_piece(0, xh * 4 + dn, 0), B_FUP, to_up)
    b_dn[1].wait_recv()
    b_fdn = send(o_piece(0, xh * 4 + up, 1), B_FDN, to_dn)
    a_up, a_dn = [[None, None], [None, None]], [[None, None], [None, None]]
    for h in (0, 1):
        for k, chip in enumerate((own_chip, partner_chip)):
            a_up[k][h] = send(o_piece(1, chip, h), A_UP + 2 * k + h, to_up)
            a_dn[k][1 - h] = send(o_piece(1, chip, 1 - h), A_DN + 2 * k + 1 - h, to_dn)

    for copy in p_x:
        copy.wait_recv()
    for t in range(2):
        rows = pl.ds(t * 128, 128)
        cos, sin = tables[t]

        def whole(part, first):
            cols = pl.ds(first, HD)
            return acc[part][0, rows, cols] + precv[part][rows, cols].astype(F32)

        def rotated(value):
            turned = jnp.concatenate([value[:, 64:], value[:, :64]], axis=1)
            return (value * cos + turned * sin).astype(BF16).astype(F32)

        k_new[rows, :] = rotated(whole(0, 0))
        v_new[rows, :] = whole(0, HD).astype(BF16).astype(F32)
        for h in range(4):
            q3[:, t * 8 + h, :] = rotated(whole(0, (h + 2) * HD))
            q3[:, t * 8 + 4 + h, :] = rotated(whole(1, h * HD))
    for copy in append:
        copy.wait()

    b_up[1].wait_recv()
    b_sib.append(send(o_block(0, xh * 4 + dn), B_SIB + 2, to_sib))
    b_x.append(send(o_block(0, xh * 4 + dn), B_X + 1, to_x))
    b_dn[0].wait_recv()
    b_sib.append(send(o_block(0, xh * 4 + up), B_SIB + 3, to_sib))
    b_x.append(send(o_block(0, xh * 4 + up), B_X + 2, to_x))

    scale = 1.0 / HD**0.5
    place = lax.broadcasted_iota(jnp.int32, (16, 128), 1)
    second = lax.broadcasted_iota(jnp.int32, (GROUP * 16, 1), 0) % 16 >= 8

    def attend(i, carry):
        base = i * GROUP
        query = q3[pl.ds(pl.multiple_of(base, GROUP), GROUP)].reshape(GROUP * 16, HD)
        query_low = query.astype(BF16)

        def spread(ref, t):
            value = ref[pl.ds(pl.multiple_of(t * 128 + base, GROUP), GROUP), :]
            return jnp.broadcast_to(
                value[:, None, :], (GROUP, 16, HD)).reshape(GROUP * 16, HD)

        new0 = jnp.sum(query * spread(k_new, 0), axis=1, keepdims=True) * scale
        new1 = jnp.sum(query * spread(k_new, 1), axis=1, keepdims=True) * scale
        new1 = jnp.where(second, new1, -jnp.inf)
        caches = [
            jnp.concatenate([held[table[base + k, j]] for j in range(8)], axis=0)
            for k in range(GROUP)
        ]
        scores = [
            lax.dot_general(
                query_low[k * 16:(k + 1) * 16], caches[k][:, :HD], (((1,), (1,)), ((), ())),
                preferred_element_type=F32)
            for k in range(GROUP)
        ]
        scores = jnp.concatenate([
            jnp.where(place < lengths[base + k], scores[k] * scale, -jnp.inf)
            for k in range(GROUP)], axis=0)
        top = jnp.maximum(jnp.max(scores, axis=1, keepdims=True), jnp.maximum(new0, new1))
        weights = jnp.exp(scores - top)
        weight0 = jnp.exp(new0 - top)
        weight1 = jnp.exp(new1 - top)
        total = jnp.sum(weights, axis=1, keepdims=True) + weight0 + weight1
        weights = weights.astype(BF16)
        numer = jnp.concatenate([
            jnp.dot(weights[k * 16:(k + 1) * 16], caches[k][:, HD:], preferred_element_type=F32)
            for k in range(GROUP)], axis=0)
        numer = numer + weight0.astype(BF16).astype(F32) * spread(v_new, 0)
        numer = numer + weight1.astype(BF16).astype(F32) * spread(v_new, 1)
        q3[pl.ds(pl.multiple_of(base, GROUP), GROUP)] = (numer / total).reshape(GROUP, 16, HD)
        return carry

    lax.fori_loop(0, 128 // GROUP, attend, 0)
    for t in range(2):
        for h in range(8):
            attn[pl.ds(t * 128, 128), pl.ds(h * HD, HD)] = q3[:, t * 8 + h, :].astype(BF16)

    halves = (pl.ds(0, 128), pl.ds(128, 128))

    def z_remote(src, dst, r, chip, h, sem, device):
        return pltpu.make_async_remote_copy(
            src_ref=src, dst_ref=dst, send_sem=z_ssem.at[r, chip, h], recv_sem=sem,
            device_id=device, device_id_type=MESH)

    def far_copy(r, chip, h):
        return z_remote(
            part.at[r, chip, halves[h]], zmid.at[r, h, chip % 2], r, chip, h,
            mid_rsem.at[r, h, chip % 2], at_z(z_up if h else z_dn))

    def near_copy(r, chip, side, h):
        rows = pl.ds(pl.multiple_of(h * 128, 128), 128)
        return z_remote(
            part.at[r, chip, rows], zrecv.at[r, side, chip % 2, rows], r, chip, h,
            z_rsem.at[r, side, chip % 2, h], at_z((z + 3 + 2 * side) % 4))

    def distance(chip):
        return (z - chip // 2 + 4) % 4

    def unit(r, chip):
        for n in range(2):
            cols = pl.ds(n * 256, 256)
            part[r, chip, :, cols] = jnp.dot(
                attn[...], wo[r, chip, :, cols], preferred_element_type=F32).astype(BF16)
        d = distance(chip)

        @pl.when(d == 2)
        def _():
            far_copy(r, chip, 0).start()
            far_copy(r, chip, 1).start()

        @pl.when(d % 2 == 1)
        def _():
            side = d // 2
            near_copy(r, chip, side, 1 - side).start()

    def late(r, chip):
        d = distance(chip)

        @pl.when(d % 2 == 1)
        def _():
            side = d // 2
            rows = pl.ds(pl.multiple_of(side * 128, 128), 128)
            landing = zmid.at[r, side, chip % 2]
            pltpu.make_async_copy(landing, landing, mid_rsem.at[r, side, chip % 2]).wait()
            part[r, chip, rows] = (
                part[r, chip, rows].astype(F32) + zmid[r, side, chip % 2].astype(F32)
            ).astype(BF16)
            near_copy(r, chip, side, side).start()

    waiting = []

    def run(r, chip):
        unit(r, chip)
        waiting.append((r, chip))
        if len(waiting) > 2:
            late(*waiting.pop(0))

    b_fup.wait_recv()
    b_x.append(send(o_piece(0, xh * 4 + opp, 0), B_X + 3, to_x))
    b_sib.append(send(o_piece(0, xh * 4 + opp, 0), B_SIB + 4, to_sib))
    b_fdn.wait_recv()
    b_x.append(send(o_piece(0, xh * 4 + opp, 1), B_X + 4, to_x))
    b_sib.append(send(o_piece(0, xh * 4 + opp, 1), B_SIB + 5, to_sib))
    a_sib[0].wait_recv()
    run(1, own_chip)
    b_sib[0].wait_recv()
    run(0, own_chip)
    a_fup, a_fdn = [], []
    for k, side in enumerate((xh, 1 - xh)):
        a_up[k][0].wait_recv()
        a_fup.append(send(o_piece(1, side * 4 + dn, 0), A_FUP + k, to_up))
        a_dn[k][1].wait_recv()
        a_fdn.append(send(o_piece(1, side * 4 + up, 1), A_FDN + k, to_dn))
    a_sib[1].wait_recv()
    run(1, partner_chip)
    b_sib[1].wait_recv()
    run(0, partner_chip)
    b_sib[2].wait_recv()
    run(0, xh * 4 + dn)
    b_sib[3].wait_recv()
    run(0, xh * 4 + up)
    b_sib[4].wait_recv()
    b_sib[5].wait_recv()
    run(0, xh * 4 + opp)

    for k, side in enumerate((xh, 1 - xh)):
        a_up[k][1].wait_recv()
        a_sib.append(send(o_block(1, side * 4 + dn), A_SIB + 2 + 2 * k, to_sib))
        a_dn[k][0].wait_recv()
        a_sib.append(send(o_block(1, side * 4 + up), A_SIB + 3 + 2 * k, to_sib))
        b_x[1 + k].wait_recv()
        chip = (1 - xh) * 4 + (dn, up)[k]
        b_sib.append(send(o_block(0, chip), B_SIB + 6 + k, to_sib))
        a_sib[2 + 2 * k].wait_recv()
        run(1, side * 4 + dn)
        a_sib[3 + 2 * k].wait_recv()
        run(1, side * 4 + up)
        b_sib[6 + k].wait_recv()
        run(0, chip)
    for h in (0, 1):
        b_x[3 + h].wait_recv()
        b_sib.append(send(o_piece(0, (1 - xh) * 4 + opp, h), B_SIB + 8 + h, to_sib))
    b_sib[8].wait_recv()
    b_sib[9].wait_recv()
    run(0, (1 - xh) * 4 + opp)
    for k, side in enumerate((xh, 1 - xh)):
        a_fup[k].wait_recv()
        a_sib.append(send(o_piece(1, side * 4 + opp, 0), A_SIB + 6 + 2 * k, to_sib))
        a_fdn[k].wait_recv()
        a_sib.append(send(o_piece(1, side * 4 + opp, 1), A_SIB + 7 + 2 * k, to_sib))
        a_sib[6 + 2 * k].wait_recv()
        a_sib[7 + 2 * k].wait_recv()
        run(1, side * 4 + opp)
        if k == 0:
            while waiting and waiting[0][0] == 0:
                late(*waiting.pop(0))
    for pair in waiting:
        late(*pair)

    def z_sum(r, lo):
        total = part[r, z * 2 + lo].astype(F32)
        for side in range(2):
            total = total + zrecv[r, side, lo].astype(F32)
        return total

    def z_wait(r, lo):
        for side in range(2):
            for h in range(2):
                landing = zrecv.at[r, side, lo, halves[h]]
                pltpu.make_async_copy(landing, landing, z_rsem.at[r, side, lo, h]).wait()

    r_x = []
    for r in range(2):
        z_wait(r, 1 - xl)
        xsend[r] = z_sum(r, 1 - xl).astype(BF16)
        r_x.append(send(xsend.at[r], R_X + r, to_lo, xrecv.at[r]))
    for r in range(2):
        z_wait(r, xl)
        r_x[r].wait_recv()
        total = (z_sum(r, xl) + xrecv[r].astype(F32)).astype(BF16)
        for core in range(2):
            out[:, pl.ds(core * 512 + r * 256, 256)] = total[:, core * 256:(core + 1) * 256]

    for copy in sent:
        copy.wait_send()
    for r in range(2):
        for chip in range(8):
            @pl.when(distance(chip) != 0)
            def _():
                for h in range(2):
                    rows = part.at[r, chip, halves[h]]
                    pltpu.make_async_copy(rows, rows, z_ssem.at[r, chip, h]).wait()


def per_device(tokens, q_weight, kv_weight, o_weight, kv_pool, send_list, page_table, lengths):
    rows = tokens.shape[1]
    hbm = pl.BlockSpec(memory_space=pl.ANY)
    vmem = pl.BlockSpec(memory_space=pltpu.VMEM)
    smem = pl.BlockSpec(memory_space=pltpu.SMEM)
    mixed = pl.pallas_call(
        kernel,
        out_shape=jax.ShapeDtypeStruct((256, 1024), BF16),
        in_specs=[hbm] * 5 + [vmem] + [smem] * 3,
        out_specs=vmem,
        scratch_shapes=[
            pltpu.VMEM((4, 1024, WIDTH[0]), BF16),
            pltpu.VMEM((4, 1024, WIDTH[1]), BF16),
            pltpu.VMEM((2, 8, 1024, 512), BF16),
            pltpu.VMEM((2, 256, 4096), BF16),
            pltpu.VMEM((1152, 16, 256), BF16),
            pltpu.VMEM((2, 64, 16, 256), BF16),
            pltpu.VMEM((64, 16, 256), BF16),
            pltpu.VMEM((2, 64, 16, 256), BF16),
            pltpu.VMEM((2, 256, WIDTH[0]), F32),
            pltpu.VMEM((2, 256, WIDTH[1]), F32),
            pltpu.VMEM((256, WIDTH[0]), BF16),
            pltpu.VMEM((256, WIDTH[1]), BF16),
            pltpu.VMEM((256, WIDTH[0]), BF16),
            pltpu.VMEM((256, WIDTH[1]), BF16),
            pltpu.VMEM((128, 16, 128), F32),
            pltpu.VMEM((256, 128), F32),
            pltpu.VMEM((256, 128), F32),
            pltpu.VMEM((256, 1024), BF16),
            pltpu.VMEM((2, 8, 256, 512), BF16),
            pltpu.VMEM((2, 2, 2, 128, 512), BF16),
            pltpu.VMEM((2, 2, 2, 256, 512), BF16),
            pltpu.VMEM((2, 256, 512), BF16),
            pltpu.VMEM((2, 256, 512), BF16),
            pltpu.SemaphoreType.DMA((N_REMOTE,)),
            pltpu.SemaphoreType.DMA((N_REMOTE,)),
            pltpu.SemaphoreType.DMA((2, 8, 2)),
            pltpu.SemaphoreType.DMA((2, 2, 2)),
            pltpu.SemaphoreType.DMA((2, 2, 2, 2)),
            pltpu.SemaphoreType.DMA((10,)),
        ],
        compiler_params=pltpu.CompilerParams(
            collective_id=0, has_side_effects=True, vmem_limit_bytes=62 * 2**20),
    )(
        tokens.reshape(2 * rows, tokens.shape[2]), q_weight, kv_weight, o_weight, kv_pool,
        lengths.reshape(1, rows), send_list, page_table, lengths,
    )
    return mixed.reshape(2, rows, -1)


def solution(mesh):
    in_specs = (
        P(None, "group", None),
        P("group", "mp"),
        P("group", "mp"),
        P("mp", "group"),
        P("group", None, "mp"),
        P("group", None, None),
        P("group", None),
        P("group"),
    )
    out_specs = P(None, "group", "mp")
    return jax.shard_map(
        per_device, mesh=mesh, in_specs=in_specs, out_specs=out_specs, check_vma=False
    )
```

```python
import jax
import jax.numpy as jnp
from jax import lax
from jax.experimental import pallas as pl
from jax.experimental.pallas import tpu as pltpu
from jax.sharding import PartitionSpec as P

HD = 128
GROUP = 16
MESH = pl.DeviceIdType.MESH
BF16 = jnp.bfloat16
F32 = jnp.float32
LOG_BASE = 13.122363377404328

Q_UP, Q_DN, Q_FUP, Q_FDN, Q_SIB = 0, 2, 4, 5, 6
T_X, T_Z, P_X, G_X, G_Y = 11, 12, 15, 16, 17
B_UP, B_DN, B_FUP, B_FDN, B_X, B_SIB = 24, 26, 28, 29, 30, 35
A_X, A_UP, A_DN, A_FUP, A_FDN, A_SIB = 45, 46, 50, 54, 56, 58
R_X = 82
N_REMOTE = 116
FIRST = (0, 256, 384)
SPAN = (256, 128, 128)
WIDTH = (768, 512)


def kernel(
    tokens, q_weight, kv_weight, o_weight, pool, row_lengths, send_list, table, lengths, out,
    wq0, wq1, wo0, wo1, wo2, tok, held, arrived, leaving, staying, acc0, acc1, psend0, psend1, precv0, precv1, q3, k_new, v_new, attn,
    part0, part1, part2, zmid0, zmid1, zmid2, zrecv0, zrecv1, zrecv2,
    xsend0, xsend1, xsend2, xrecv0, xrecv1, xrecv2,
    ssem, rsem, z_ssem, mid_rsem, z_rsem, lsem,
):
    g = lax.axis_index("group")
    m = lax.axis_index("mp")
    wq, acc, psend, precv = (wq0, wq1), (acc0, acc1), (psend0, psend1), (precv0, precv1)
    wo, part, zmid = (wo0, wo1, wo2), (part0, part1, part2), (zmid0, zmid1, zmid2)
    zrecv, xsend, xrecv = (zrecv0, zrecv1, zrecv2), (xsend0, xsend1, xsend2), (xrecv0, xrecv1, xrecv2)
    xh, y, c = g // 8, (g // 2) % 4, g % 2
    z, xl = m // 2, m % 2
    up, dn, opp = (y + 1) % 4, (y + 3) % 4, (y + 2) % 4
    z_up, z_dn = (z + 1) % 4, (z + 3) % 4
    me = y * 2 + c

    def in_group(xh_, y_, c_):
        return (xh_ * 8 + y_ * 2 + c_, m)

    to_up, to_dn = in_group(xh, up, c), in_group(xh, dn, c)
    to_x, to_sib = in_group(1 - xh, y, c), in_group(xh, y, 1 - c)
    to_lo = (g, z * 2 + 1 - xl)

    def at_z(z_):
        return (g, z_ * 2 + xl)

    half = pl.multiple_of(xh * 4096, 4096)
    other_half = pl.multiple_of((1 - xh) * 4096, 4096)
    my_rows = pl.ds(pl.multiple_of(c * 512, 512), 512)
    my_cols = [pl.ds(pl.multiple_of(c * span, span), span) for span in SPAN]
    own_chip, partner_chip = xh * 4 + y, (1 - xh) * 4 + y
    loads = [
        pltpu.make_async_copy(kv_weight, wq0.at[y, my_rows, pl.ds(0, 256)], lsem.at[0]),
        pltpu.make_async_copy(
            q_weight.at[:, pl.ds(0, 512)], wq0.at[y, my_rows, pl.ds(256, 512)], lsem.at[1]),
        pltpu.make_async_copy(q_weight.at[:, pl.ds(512, 512)], wq1.at[y, my_rows], lsem.at[9]),
        pltpu.make_async_copy(pool, held.at[pl.ds(0, 1024)], lsem.at[2]),
        pltpu.make_async_copy(tokens.at[:, pl.ds(half, 4096)], tok.at[0], lsem.at[5]),
    ]
    o_loads = [
        pltpu.make_async_copy(
            o_weight.at[:, pl.ds(FIRST[r], SPAN[r])], wo[r].at[own_chip, :, my_cols[r]],
            lsem.at[10 + r])
        for r in range(3)
    ]
    for load in loads + o_loads:
        load.start()

    barrier = pltpu.get_barrier_semaphore()
    for off in range(1, 8):
        pl.semaphore_signal(
            barrier, inc=1, device_id=(xh * 8 + (me + off) % 8, m), device_id_type=MESH)
    for off in range(1, 4):
        pl.semaphore_signal(barrier, inc=1, device_id=at_z((z + off) % 4), device_id_type=MESH)
    pl.semaphore_signal(barrier, inc=1, device_id=to_x, device_id_type=MESH)
    pl.semaphore_signal(barrier, inc=1, device_id=to_lo, device_id_type=MESH)
    pl.semaphore_wait(barrier, 12)

    sent = []

    def send(ref, number, device, there=None):
        copy = pltpu.make_async_remote_copy(
            src_ref=ref, dst_ref=ref if there is None else there,
            send_sem=ssem.at[number], recv_sem=rsem.at[number],
            device_id=device, device_id_type=MESH,
        )
        copy.start()
        sent.append(copy)
        return copy

    my_quarter = pl.ds(pl.multiple_of(z * 64, 64), 64)
    t_x = send(
        tokens.at[my_quarter, pl.ds(other_half, 4096)], T_X, to_x, tok.at[1, my_quarter])

    def q_piece(part, yy, h):
        return wq[part].at[yy, pl.ds(pl.multiple_of(c * 512 + h * 256, 256), 256)]

    def q_block(part, yy):
        return wq[part].at[yy, my_rows]

    q_up, q_dn, q_sib = [[None, None], [None, None]], [[None, None], [None, None]], [[], []]

    def q_send(part):
        for h in (0, 1):
            q_up[part][h] = send(q_piece(part, y, h), 70 * part + Q_UP + h, to_up)
            q_dn[part][1 - h] = send(q_piece(part, y, 1 - h), 70 * part + Q_DN + 1 - h, to_dn)
        q_sib[part].append(send(q_block(part, y), 70 * part + Q_SIB, to_sib))

    q_fup, q_fdn = [None, None], [None, None]

    def q_forward(part):
        q_up[part][0].wait_recv()
        q_fup[part] = send(q_piece(part, dn, 0), 70 * part + Q_FUP, to_up)
        q_dn[part][1].wait_recv()
        q_fdn[part] = send(q_piece(part, up, 1), 70 * part + Q_FDN, to_dn)

    def q_near(part):
        q_up[part][1].wait_recv()
        q_sib[part].append(send(q_block(part, dn), 70 * part + Q_SIB + 1, to_sib))
        q_dn[part][0].wait_recv()
        q_sib[part].append(send(q_block(part, up), 70 * part + Q_SIB + 2, to_sib))

    def q_far(part):
        q_fup[part].wait_recv()
        q_sib[part].append(send(q_piece(part, opp, 0), 70 * part + Q_SIB + 3, to_sib))
        q_fdn[part].wait_recv()
        q_sib[part].append(send(q_piece(part, opp, 1), 70 * part + Q_SIB + 4, to_sib))

    loads[0].wait()
    loads[1].wait()
    q_send(0)

    loads[3].wait()

    def gather_pages(i, carry):
        for k in range(8):
            leaving[i * 8 + k] = held[send_list[0, (1 - xh) * 8 + i, k]]
            staying[xh, i * 8 + k] = held[send_list[0, xh * 8 + i, k]]
        return carry

    lax.fori_loop(0, 8, gather_pages, 0)

    t_x.wait_recv()
    t_z = []
    for off in range(1, 4):
        t_z.append(send(tok.at[1, my_quarter], T_Z + off - 1, at_z((z + off) % 4)))

    g_x = send(leaving, G_X, to_x, staying.at[xh])

    def o_block(r, chip):
        return wo[r].at[chip, :, my_cols[r]]

    def o_piece(r, chip, h):
        return wo[r].at[chip, pl.ds(h * 512, 512), my_cols[r]]

    q_forward(0)
    loads[2].wait()
    q_send(1)
    for load in o_loads:
        load.wait()
    a_x, a_sib = {}, {}
    for r in (1, 2):
        a_x[r] = send(o_block(r, own_chip), A_X + 45 * (r - 1), to_x)
        a_sib[r] = [send(o_block(r, own_chip), A_SIB + 45 * (r - 1), to_sib)]
    b_x = [send(o_block(0, own_chip), B_X, to_x)]
    b_sib = [send(o_block(0, own_chip), B_SIB, to_sib)]

    def project(part, which, yy, first=False):
        left = pl.ds(pl.multiple_of(yy * 1024, 1024), 1024)

        def step(n, carry):
            cols = pl.ds(pl.multiple_of(n * 256, 256), 256)
            product = jnp.dot(
                tok[which, :, left], wq[part][yy, :, cols], preferred_element_type=F32)
            acc[part][which, :, cols] = (
                product if first else acc[part][which, :, cols] + product)
            return carry

        lax.fori_loop(0, WIDTH[part] // 256, step, 0)

    loads[4].wait()
    q_sib[0][0].wait_recv()
    project(0, 0, y, True)
    q_near(0)
    q_sib[0][1].wait_recv()
    project(0, 0, dn)
    q_sib[0][2].wait_recv()
    project(0, 0, up)
    q_forward(1)
    q_far(0)

    for copy in t_z:
        copy.wait_recv()
    project(0, 1, y, True)
    project(0, 1, dn)
    project(0, 1, up)
    q_sib[0][3].wait_recv()
    q_sib[0][4].wait_recv()
    project(0, 1, opp)
    psend0[...] = acc0[1].astype(BF16)
    p_x = [send(psend0, P_X, to_x, precv0)]

    q_near(1)
    q_sib[1][0].wait_recv()
    project(1, 1, y, True)
    project(1, 0, y, True)
    q_sib[1][1].wait_recv()
    project(1, 1, dn)
    q_sib[1][2].wait_recv()
    project(1, 1, up)
    q_far(1)

    g_x.wait_recv()
    g_y = []
    my_slot = pl.ds(pl.multiple_of(me * 8, 8), 8)
    for off in range(1, 8):
        there = (me + off) % 8
        slot = pl.ds(pl.multiple_of(there * 8, 8), 8)
        g_y.append(send(
            staying.at[:, slot], G_Y + off - 1, (xh * 8 + there, m), arrived.at[:, my_slot]))
    own_pages = pltpu.make_async_copy(
        staying.at[:, my_slot], arrived.at[:, my_slot], lsem.at[6])
    own_pages.start()
    b_up, b_dn = [None, None], [None, None]
    for h in (0, 1):
        b_up[h] = send(o_piece(0, own_chip, h), B_UP + h, to_up)
        b_dn[1 - h] = send(o_piece(0, own_chip, 1 - h), B_DN + 1 - h, to_dn)

    q_sib[1][3].wait_recv()
    q_sib[1][4].wait_recv()
    project(1, 1, opp)
    psend1[...] = acc1[1].astype(BF16)
    p_x.append(send(psend1, P_X + 70, to_x, precv1))
    project(0, 0, opp)
    project(1, 0, dn)
    project(1, 0, up)
    project(1, 0, opp)

    for r in (1, 2):
        a_x[r].wait_recv()
        a_sib[r].append(send(o_block(r, partner_chip), A_SIB + 1 + 45 * (r - 1), to_sib))
    b_x[0].wait_recv()
    b_sib.append(send(o_block(0, partner_chip), B_SIB + 1, to_sib))

    diagonal = (
        lax.broadcasted_iota(jnp.int32, (128, 128), 0)
        == lax.broadcasted_iota(jnp.int32, (128, 128), 1))
    lane = lax.broadcasted_iota(jnp.int32, (1, 128), 1)
    inverse = jnp.exp((lane % 64).astype(F32) * (-2.0 / 128.0 * LOG_BASE))
    position = jnp.sum(
        jnp.where(diagonal, row_lengths[...].astype(F32), 0.0), axis=1, keepdims=True)
    tables = []
    for t in range(2):
        angle = (position + float(t)) * inverse
        tables.append((jnp.cos(angle), jnp.where(lane < 64, -1.0, 1.0) * jnp.sin(angle)))

    for copy in g_y:
        copy.wait_recv()
    own_pages.wait()
    append = [
        pltpu.make_async_copy(
            arrived.at[k], held.at[pl.ds(1024 + 64 * k, 64)], lsem.at[7 + k])
        for k in range(2)
    ]
    for copy in append:
        copy.start()

    b_up[0].wait_recv()
    b_fup = send(o_piece(0, xh * 4 + dn, 0), B_FUP, to_up)
    b_dn[1].wait_recv()
    b_fdn = send(o_piece(0, xh * 4 + up, 1), B_FDN, to_dn)
    a_up, a_dn, a_fup, a_fdn = {}, {}, {}, {}

    def a_send(r):
        for h in (0, 1):
            for k, chip in enumerate((own_chip, partner_chip)):
                first = 45 * (r - 1) + 2 * k
                a_up[r, k, h] = send(o_piece(r, chip, h), A_UP + first + h, to_up)
                a_dn[r, k, 1 - h] = send(o_piece(r, chip, 1 - h), A_DN + first + 1 - h, to_dn)

    def a_forward(r):
        for k, side in enumerate((xh, 1 - xh)):
            a_up[r, k, 0].wait_recv()
            a_fup[r, k] = send(
                o_piece(r, side * 4 + dn, 0), A_FUP + 45 * (r - 1) + k, to_up)
            a_dn[r, k, 1].wait_recv()
            a_fdn[r, k] = send(
                o_piece(r, side * 4 + up, 1), A_FDN + 45 * (r - 1) + k, to_dn)

    def a_near(r):
        for k, side in enumerate((xh, 1 - xh)):
            first = A_SIB + 45 * (r - 1) + 2 + 2 * k
            a_up[r, k, 1].wait_recv()
            a_sib[r].append(send(o_block(r, side * 4 + dn), first, to_sib))
            a_dn[r, k, 0].wait_recv()
            a_sib[r].append(send(o_block(r, side * 4 + up), first + 1, to_sib))

    def a_far(r):
        for k, side in enumerate((xh, 1 - xh)):
            first = A_SIB + 45 * (r - 1) + 6 + 2 * k
            a_fup[r, k].wait_recv()
            a_sib[r].append(send(o_piece(r, side * 4 + opp, 0), first, to_sib))
            a_fdn[r, k].wait_recv()
            a_sib[r].append(send(o_piece(r, side * 4 + opp, 1), first + 1, to_sib))

    a_send(1)

    for copy in p_x:
        copy.wait_recv()
    for t in range(2):
        rows = pl.ds(t * 128, 128)
        cos, sin = tables[t]

        def whole(part, first):
            cols = pl.ds(first, HD)
            return acc[part][0, rows, cols] + precv[part][rows, cols].astype(F32)

        def rotated(value):
            turned = jnp.concatenate([value[:, 64:], value[:, :64]], axis=1)
            return (value * cos + turned * sin).astype(BF16).astype(F32)

        k_new[rows, :] = rotated(whole(0, 0))
        v_new[rows, :] = whole(0, HD).astype(BF16).astype(F32)
        for h in range(4):
            q3[:, t * 8 + h, :] = rotated(whole(0, (h + 2) * HD))
            q3[:, t * 8 + 4 + h, :] = rotated(whole(1, h * HD))
    for copy in append:
        copy.wait()

    b_up[1].wait_recv()
    b_sib.append(send(o_block(0, xh * 4 + dn), B_SIB + 2, to_sib))
    b_x.append(send(o_block(0, xh * 4 + dn), B_X + 1, to_x))
    b_dn[0].wait_recv()
    b_sib.append(send(o_block(0, xh * 4 + up), B_SIB + 3, to_sib))
    b_x.append(send(o_block(0, xh * 4 + up), B_X + 2, to_x))

    scale = 1.0 / HD**0.5
    place = lax.broadcasted_iota(jnp.int32, (16, 128), 1)
    second = lax.broadcasted_iota(jnp.int32, (GROUP * 16, 1), 0) % 16 >= 8

    def attend(i, carry):
        base = i * GROUP
        query = q3[pl.ds(pl.multiple_of(base, GROUP), GROUP)].reshape(GROUP * 16, HD)
        query_low = query.astype(BF16)

        def spread(ref, t):
            value = ref[pl.ds(pl.multiple_of(t * 128 + base, GROUP), GROUP), :]
            return jnp.broadcast_to(
                value[:, None, :], (GROUP, 16, HD)).reshape(GROUP * 16, HD)

        new0 = jnp.sum(query * spread(k_new, 0), axis=1, keepdims=True) * scale
        new1 = jnp.sum(query * spread(k_new, 1), axis=1, keepdims=True) * scale
        new1 = jnp.where(second, new1, -jnp.inf)
        caches = [
            jnp.concatenate([held[table[base + k, j]] for j in range(8)], axis=0)
            for k in range(GROUP)
        ]
        scores = [
            lax.dot_general(
                query_low[k * 16:(k + 1) * 16], caches[k][:, :HD], (((1,), (1,)), ((), ())),
                preferred_element_type=F32)
            for k in range(GROUP)
        ]
        scores = jnp.concatenate([
            jnp.where(place < lengths[base + k], scores[k] * scale, -jnp.inf)
            for k in range(GROUP)], axis=0)
        top = jnp.maximum(jnp.max(scores, axis=1, keepdims=True), jnp.maximum(new0, new1))
        weights = jnp.exp(scores - top)
        weight0 = jnp.exp(new0 - top)
        weight1 = jnp.exp(new1 - top)
        total = jnp.sum(weights, axis=1, keepdims=True) + weight0 + weight1
        weights = weights.astype(BF16)
        numer = jnp.concatenate([
            jnp.dot(weights[k * 16:(k + 1) * 16], caches[k][:, HD:], preferred_element_type=F32)
            for k in range(GROUP)], axis=0)
        numer = numer + weight0.astype(BF16).astype(F32) * spread(v_new, 0)
        numer = numer + weight1.astype(BF16).astype(F32) * spread(v_new, 1)
        q3[pl.ds(pl.multiple_of(base, GROUP), GROUP)] = (numer / total).reshape(GROUP, 16, HD)
        return carry

    lax.fori_loop(0, 128 // GROUP, attend, 0)
    for t in range(2):
        for h in range(8):
            attn[pl.ds(t * 128, 128), pl.ds(h * HD, HD)] = q3[:, t * 8 + h, :].astype(BF16)

    halves = (pl.ds(0, 128), pl.ds(128, 128))

    def z_remote(src, dst, r, chip, h, sem, device):
        return pltpu.make_async_remote_copy(
            src_ref=src, dst_ref=dst, send_sem=z_ssem.at[r, chip, h], recv_sem=sem,
            device_id=device, device_id_type=MESH)

    def far_copy(r, chip, h):
        return z_remote(
            part[r].at[chip, halves[h]], zmid[r].at[h, chip % 2], r, chip, h,
            mid_rsem.at[r, h, chip % 2], at_z(z_up if h else z_dn))

    def near_copy(r, chip, side, h):
        rows = pl.ds(pl.multiple_of(h * 128, 128), 128)
        return z_remote(
            part[r].at[chip, rows], zrecv[r].at[side, chip % 2, rows], r, chip, h,
            z_rsem.at[r, side, chip % 2, h], at_z((z + 3 + 2 * side) % 4))

    def distance(chip):
        return (z - chip // 2 + 4) % 4

    def unit(r, chip):
        for n in range(SPAN[r] // 128):
            cols = pl.ds(n * 256, 256)
            part[r][chip, :, cols] = jnp.dot(
                attn[...], wo[r][chip, :, cols], preferred_element_type=F32).astype(BF16)
        d = distance(chip)

        @pl.when(d == 2)
        def _():
            far_copy(r, chip, 0).start()
            far_copy(r, chip, 1).start()

        @pl.when(d % 2 == 1)
        def _():
            side = d // 2
            near_copy(r, chip, side, 1 - side).start()

    def late(r, chip):
        d = distance(chip)

        @pl.when(d % 2 == 1)
        def _():
            side = d // 2
            rows = pl.ds(pl.multiple_of(side * 128, 128), 128)
            landing = zmid[r].at[side, chip % 2]
            pltpu.make_async_copy(landing, landing, mid_rsem.at[r, side, chip % 2]).wait()
            part[r][chip, rows] = (
                part[r][chip, rows].astype(F32) + zmid[r][side, chip % 2].astype(F32)
            ).astype(BF16)
            near_copy(r, chip, side, side).start()

    waiting = []

    def run(r, chip):
        unit(r, chip)
        waiting.append((r, chip))
        if len(waiting) > 5:
            late(*waiting.pop(0))

    b_fup.wait_recv()
    b_x.append(send(o_piece(0, xh * 4 + opp, 0), B_X + 3, to_x))
    b_sib.append(send(o_piece(0, xh * 4 + opp, 0), B_SIB + 4, to_sib))
    b_fdn.wait_recv()
    b_x.append(send(o_piece(0, xh * 4 + opp, 1), B_X + 4, to_x))
    b_sib.append(send(o_piece(0, xh * 4 + opp, 1), B_SIB + 5, to_sib))
    for r in (1, 2):
        a_sib[r][0].wait_recv()
        run(r, own_chip)
    b_sib[0].wait_recv()
    run(0, own_chip)
    a_forward(1)
    a_send(2)
    for r in (1, 2):
        a_sib[r][1].wait_recv()
        run(r, partner_chip)
    b_sib[1].wait_recv()
    run(0, partner_chip)
    b_sib[2].wait_recv()
    run(0, xh * 4 + dn)
    b_sib[3].wait_recv()
    run(0, xh * 4 + up)
    a_near(1)
    b_sib[4].wait_recv()
    b_sib[5].wait_recv()
    run(0, xh * 4 + opp)

    def run_near(r):
        for k, side in enumerate((xh, 1 - xh)):
            a_sib[r][2 + 2 * k].wait_recv()
            run(r, side * 4 + dn)
            a_sib[r][3 + 2 * k].wait_recv()
            run(r, side * 4 + up)

    def run_far(r):
        for k, side in enumerate((xh, 1 - xh)):
            a_sib[r][6 + 2 * k].wait_recv()
            a_sib[r][7 + 2 * k].wait_recv()
            run(r, side * 4 + opp)

    def flush(left):
        while len(waiting) > left:
            late(*waiting.pop(0))

    def z_sum(r, lo):
        total = part[r][z * 2 + lo].astype(F32)
        for side in range(2):
            total = total + zrecv[r][side, lo].astype(F32)
        return total

    def z_wait(r, lo):
        for side in range(2):
            for h in range(2):
                landing = zrecv[r].at[side, lo, halves[h]]
                pltpu.make_async_copy(landing, landing, z_rsem.at[r, side, lo, h]).wait()

    r_x = {}

    def reduce_other(r):
        z_wait(r, 1 - xl)
        xsend[r][...] = z_sum(r, 1 - xl).astype(BF16)
        r_x[r] = send(xsend[r], R_X + r, to_lo, xrecv[r])

    def reduce_own(r):
        z_wait(r, xl)
        r_x[r].wait_recv()
        total = (z_sum(r, xl) + xrecv[r][...].astype(F32)).astype(BF16)
        for core in range(2):
            out[:, pl.ds(core * 512 + FIRST[r], SPAN[r])] = (
                total[:, core * SPAN[r]:(core + 1) * SPAN[r]])

    run_near(1)
    for k, chip in enumerate(((1 - xh) * 4 + dn, (1 - xh) * 4 + up)):
        b_x[1 + k].wait_recv()
        b_sib.append(send(o_block(0, chip), B_SIB + 6 + k, to_sib))
    a_far(1)
    a_forward(2)
    for k, chip in enumerate(((1 - xh) * 4 + dn, (1 - xh) * 4 + up)):
        b_sib[6 + k].wait_recv()
        run(0, chip)
    run_far(1)
    for h in (0, 1):
        b_x[3 + h].wait_recv()
        b_sib.append(send(o_piece(0, (1 - xh) * 4 + opp, h), B_SIB + 8 + h, to_sib))
    a_near(2)
    b_sib[8].wait_recv()
    b_sib[9].wait_recv()
    run(0, (1 - xh) * 4 + opp)
    run_near(2)
    flush(4)
    a_far(2)
    run_far(2)
    flush(2)
    reduce_other(1)
    reduce_other(0)
    flush(0)
    reduce_other(2)
    reduce_own(1)
    reduce_own(0)
    reduce_own(2)

    for copy in sent:
        copy.wait_send()
    for r in range(3):
        for chip in range(8):
            @pl.when(distance(chip) != 0)
            def _():
                for h in range(2):
                    rows = part[r].at[chip, halves[h]]
                    pltpu.make_async_copy(rows, rows, z_ssem.at[r, chip, h]).wait()


def per_device(tokens, q_weight, kv_weight, o_weight, kv_pool, send_list, page_table, lengths):
    rows = tokens.shape[1]
    hbm = pl.BlockSpec(memory_space=pl.ANY)
    vmem = pl.BlockSpec(memory_space=pltpu.VMEM)
    smem = pl.BlockSpec(memory_space=pltpu.SMEM)
    mixed = pl.pallas_call(
        kernel,
        out_shape=jax.ShapeDtypeStruct((256, 1024), BF16),
        in_specs=[hbm] * 5 + [vmem] + [smem] * 3,
        out_specs=vmem,
        scratch_shapes=[
            pltpu.VMEM((4, 1024, WIDTH[0]), BF16),
            pltpu.VMEM((4, 1024, WIDTH[1]), BF16),
            *[pltpu.VMEM((8, 1024, 2 * span), BF16) for span in SPAN],
            pltpu.VMEM((2, 256, 4096), BF16),
            pltpu.VMEM((1152, 16, 256), BF16),
            pltpu.VMEM((2, 64, 16, 256), BF16),
            pltpu.VMEM((64, 16, 256), BF16),
            pltpu.VMEM((2, 64, 16, 256), BF16),
            pltpu.VMEM((2, 256, WIDTH[0]), F32),
            pltpu.VMEM((2, 256, WIDTH[1]), F32),
            pltpu.VMEM((256, WIDTH[0]), BF16),
            pltpu.VMEM((256, WIDTH[1]), BF16),
            pltpu.VMEM((256, WIDTH[0]), BF16),
            pltpu.VMEM((256, WIDTH[1]), BF16),
            pltpu.VMEM((128, 16, 128), F32),
            pltpu.VMEM((256, 128), F32),
            pltpu.VMEM((256, 128), F32),
            pltpu.VMEM((256, 1024), BF16),
            *[pltpu.VMEM((8, 256, 2 * span), BF16) for span in SPAN],
            *[pltpu.VMEM((2, 2, 128, 2 * span), BF16) for span in SPAN],
            *[pltpu.VMEM((2, 2, 256, 2 * span), BF16) for span in SPAN],
            *[pltpu.VMEM((256, 2 * span), BF16) for span in SPAN * 2],
            pltpu.SemaphoreType.DMA((N_REMOTE,)),
            pltpu.SemaphoreType.DMA((N_REMOTE,)),
            pltpu.SemaphoreType.DMA((3, 8, 2)),
            pltpu.SemaphoreType.DMA((3, 2, 2)),
            pltpu.SemaphoreType.DMA((3, 2, 2, 2)),
            pltpu.SemaphoreType.DMA((13,)),
        ],
        compiler_params=pltpu.CompilerParams(
            collective_id=0, has_side_effects=True, vmem_limit_bytes=62 * 2**20),
    )(
        tokens.reshape(2 * rows, tokens.shape[2]), q_weight, kv_weight, o_weight, kv_pool,
        lengths.reshape(1, rows), send_list, page_table, lengths,
    )
    return mixed.reshape(2, rows, -1)


def solution(mesh):
    in_specs = (
        P(None, "group", None),
        P("group", "mp"),
        P("group", "mp"),
        P("mp", "group"),
        P("group", None, "mp"),
        P("group", None, None),
        P("group", None),
        P("group"),
    )
    out_specs = P(None, "group", "mp")
    return jax.shard_map(
        per_device, mesh=mesh, in_specs=in_specs, out_specs=out_specs, check_vma=False
    )
```

```python
import jax
import jax.numpy as jnp
from jax import lax
from jax.experimental import pallas as pl
from jax.experimental.pallas import tpu as pltpu
from jax.sharding import PartitionSpec as P

HD = 128
GROUP = 16
MESH = pl.DeviceIdType.MESH
BF16 = jnp.bfloat16
F32 = jnp.float32
LOG_BASE = 13.122363377404328

Q_UP, Q_DN, Q_FUP, Q_FDN, Q_SIB = 0, 2, 4, 5, 6
T_X, T_Z, P_X, G_X, G_Y = 11, 12, 15, 16, 17
B_UP, B_DN, B_FUP, B_FDN, B_X, B_SIB = 24, 26, 28, 29, 30, 35
A_X, A_UP, A_DN, A_FUP, A_FDN, A_SIB = 45, 46, 50, 54, 56, 58
R_X = 82
N_REMOTE = 116
FIRST = (0, 256, 384)
SPAN = (256, 128, 128)
WIDTH = (768, 512)


def kernel(
    tokens, q_weight, kv_weight, o_weight, pool, row_lengths, send_list, table, lengths, out,
    wq0, wq1, wo0, wo1, wo2, tok, held, arrived, leaving, staying, acc0, acc1, psend0, psend1, precv0, precv1, q3, k_new, v_new, attn,
    part0, part1, part2, zmid0, zmid1, zmid2, zrecv0, zrecv1, zrecv2,
    xsend0, xsend1, xsend2, xrecv0, xrecv1, xrecv2,
    ssem, rsem, z_ssem, mid_rsem, z_rsem, lsem,
):
    g = lax.axis_index("group")
    m = lax.axis_index("mp")
    wq, acc, psend, precv = (wq0, wq1), (acc0, acc1), (psend0, psend1), (precv0, precv1)
    wo, part, zmid = (wo0, wo1, wo2), (part0, part1, part2), (zmid0, zmid1, zmid2)
    zrecv, xsend, xrecv = (zrecv0, zrecv1, zrecv2), (xsend0, xsend1, xsend2), (xrecv0, xrecv1, xrecv2)
    xh, y, c = g // 8, (g // 2) % 4, g % 2
    z, xl = m // 2, m % 2
    up, dn, opp = (y + 1) % 4, (y + 3) % 4, (y + 2) % 4
    z_up, z_dn = (z + 1) % 4, (z + 3) % 4
    me = y * 2 + c

    def in_group(xh_, y_, c_):
        return (xh_ * 8 + y_ * 2 + c_, m)

    to_up, to_dn = in_group(xh, up, c), in_group(xh, dn, c)
    to_x, to_sib = in_group(1 - xh, y, c), in_group(xh, y, 1 - c)
    to_lo = (g, z * 2 + 1 - xl)

    def at_z(z_):
        return (g, z_ * 2 + xl)

    half = pl.multiple_of(xh * 4096, 4096)
    other_half = pl.multiple_of((1 - xh) * 4096, 4096)
    my_rows = pl.ds(pl.multiple_of(c * 512, 512), 512)
    own_chip, partner_chip = xh * 4 + y, (1 - xh) * 4 + y
    loads = [
        pltpu.make_async_copy(kv_weight, wq0.at[y, my_rows, pl.ds(0, 256)], lsem.at[0]),
        pltpu.make_async_copy(
            q_weight.at[:, pl.ds(0, 512)], wq0.at[y, my_rows, pl.ds(256, 512)], lsem.at[1]),
        pltpu.make_async_copy(q_weight.at[:, pl.ds(512, 512)], wq1.at[y, my_rows], lsem.at[9]),
        pltpu.make_async_copy(pool, held.at[pl.ds(0, 1024)], lsem.at[2]),
        pltpu.make_async_copy(tokens.at[:, pl.ds(half, 4096)], tok.at[0], lsem.at[5]),
    ]
    o_loads = [
        pltpu.make_async_copy(
            o_weight.at[:, pl.ds(FIRST[r], SPAN[r])], wo[r].at[own_chip, c],
            lsem.at[10 + r])
        for r in range(3)
    ]
    for load in loads + o_loads:
        load.start()

    barrier = pltpu.get_barrier_semaphore()
    for off in range(1, 8):
        pl.semaphore_signal(
            barrier, inc=1, device_id=(xh * 8 + (me + off) % 8, m), device_id_type=MESH)
    for off in range(1, 4):
        pl.semaphore_signal(barrier, inc=1, device_id=at_z((z + off) % 4), device_id_type=MESH)
    pl.semaphore_signal(barrier, inc=1, device_id=to_x, device_id_type=MESH)
    pl.semaphore_signal(barrier, inc=1, device_id=to_lo, device_id_type=MESH)
    pl.semaphore_wait(barrier, 12)

    sent = []

    def send(ref, number, device, there=None):
        copy = pltpu.make_async_remote_copy(
            src_ref=ref, dst_ref=ref if there is None else there,
            send_sem=ssem.at[number], recv_sem=rsem.at[number],
            device_id=device, device_id_type=MESH,
        )
        copy.start()
        sent.append(copy)
        return copy

    my_quarter = pl.ds(pl.multiple_of(z * 64, 64), 64)
    t_x = send(
        tokens.at[my_quarter, pl.ds(other_half, 4096)], T_X, to_x, tok.at[1, my_quarter])

    def q_piece(part, yy, h):
        return wq[part].at[yy, pl.ds(pl.multiple_of(c * 512 + h * 256, 256), 256)]

    def q_block(part, yy):
        return wq[part].at[yy, my_rows]

    q_up, q_dn, q_sib = [[None, None], [None, None]], [[None, None], [None, None]], [[], []]

    def q_send(part):
        for h in (0, 1):
            q_up[part][h] = send(q_piece(part, y, h), 70 * part + Q_UP + h, to_up)
            q_dn[part][1 - h] = send(q_piece(part, y, 1 - h), 70 * part + Q_DN + 1 - h, to_dn)
        q_sib[part].append(send(q_block(part, y), 70 * part + Q_SIB, to_sib))

    q_fup, q_fdn = [None, None], [None, None]

    def q_forward(part):
        q_up[part][0].wait_recv()
        q_fup[part] = send(q_piece(part, dn, 0), 70 * part + Q_FUP, to_up)
        q_dn[part][1].wait_recv()
        q_fdn[part] = send(q_piece(part, up, 1), 70 * part + Q_FDN, to_dn)

    def q_near(part):
        q_up[part][1].wait_recv()
        q_sib[part].append(send(q_block(part, dn), 70 * part + Q_SIB + 1, to_sib))
        q_dn[part][0].wait_recv()
        q_sib[part].append(send(q_block(part, up), 70 * part + Q_SIB + 2, to_sib))

    def q_far(part):
        q_fup[part].wait_recv()
        q_sib[part].append(send(q_piece(part, opp, 0), 70 * part + Q_SIB + 3, to_sib))
        q_fdn[part].wait_recv()
        q_sib[part].append(send(q_piece(part, opp, 1), 70 * part + Q_SIB + 4, to_sib))

    loads[0].wait()
    loads[1].wait()
    q_send(0)

    loads[3].wait()

    def gather_pages(i, carry):
        for k in range(8):
            leaving[i * 8 + k] = held[send_list[0, (1 - xh) * 8 + i, k]]
            staying[xh, i * 8 + k] = held[send_list[0, xh * 8 + i, k]]
        return carry

    lax.fori_loop(0, 8, gather_pages, 0)

    t_x.wait_recv()
    t_z = []
    for off in range(1, 4):
        t_z.append(send(tok.at[1, my_quarter], T_Z + off - 1, at_z((z + off) % 4)))

    g_x = send(leaving, G_X, to_x, staying.at[xh])

    def o_block(r, chip):
        return wo[r].at[chip, c]

    def o_piece(r, chip, h):
        return wo[r].at[chip, c, pl.ds(h * 512, 512)]

    q_forward(0)
    loads[2].wait()
    q_send(1)
    for load in o_loads:
        load.wait()
    a_x, a_sib = {}, {}
    for r in (1, 2):
        a_x[r] = send(o_block(r, own_chip), A_X + 45 * (r - 1), to_x)
        a_sib[r] = [send(o_block(r, own_chip), A_SIB + 45 * (r - 1), to_sib)]
    b_x = [send(o_block(0, own_chip), B_X, to_x)]
    b_sib = [send(o_block(0, own_chip), B_SIB, to_sib)]

    def project(part, which, yy, first=False):
        left = pl.ds(pl.multiple_of(yy * 1024, 1024), 1024)

        def step(n, carry):
            cols = pl.ds(pl.multiple_of(n * 256, 256), 256)
            product = jnp.dot(
                tok[which, :, left], wq[part][yy, :, cols], preferred_element_type=F32)
            acc[part][which, :, cols] = (
                product if first else acc[part][which, :, cols] + product)
            return carry

        lax.fori_loop(0, WIDTH[part] // 256, step, 0)

    loads[4].wait()
    q_sib[0][0].wait_recv()
    project(0, 0, y, True)
    q_near(0)
    q_sib[0][1].wait_recv()
    project(0, 0, dn)
    q_sib[0][2].wait_recv()
    project(0, 0, up)
    q_forward(1)
    q_far(0)

    for copy in t_z:
        copy.wait_recv()
    project(0, 1, y, True)
    project(0, 1, dn)
    project(0, 1, up)
    q_sib[0][3].wait_recv()
    q_sib[0][4].wait_recv()
    project(0, 1, opp)
    psend0[...] = acc0[1].astype(BF16)
    p_x = [send(psend0, P_X, to_x, precv0)]

    q_near(1)
    q_sib[1][0].wait_recv()
    project(1, 1, y, True)
    project(1, 0, y, True)
    q_sib[1][1].wait_recv()
    project(1, 1, dn)
    q_sib[1][2].wait_recv()
    project(1, 1, up)
    g_x.wait_recv()
    g_y = []
    my_slot = pl.ds(pl.multiple_of(me * 8, 8), 8)
    for off in range(1, 8):
        there = (me + off) % 8
        slot = pl.ds(pl.multiple_of(there * 8, 8), 8)
        g_y.append(send(
            staying.at[:, slot], G_Y + off - 1, (xh * 8 + there, m), arrived.at[:, my_slot]))
    own_pages = pltpu.make_async_copy(
        staying.at[:, my_slot], arrived.at[:, my_slot], lsem.at[6])
    own_pages.start()
    b_up, b_dn = [None, None], [None, None]
    for h in (0, 1):
        b_up[h] = send(o_piece(0, own_chip, h), B_UP + h, to_up)
        b_dn[1 - h] = send(o_piece(0, own_chip, 1 - h), B_DN + 1 - h, to_dn)

    q_far(1)

    q_sib[1][3].wait_recv()
    q_sib[1][4].wait_recv()
    project(1, 1, opp)
    psend1[...] = acc1[1].astype(BF16)
    p_x.append(send(psend1, P_X + 70, to_x, precv1))
    project(0, 0, opp)
    project(1, 0, dn)
    project(1, 0, up)
    project(1, 0, opp)

    for r in (1, 2):
        a_x[r].wait_recv()
        a_sib[r].append(send(o_block(r, partner_chip), A_SIB + 1 + 45 * (r - 1), to_sib))
    b_x[0].wait_recv()
    b_sib.append(send(o_block(0, partner_chip), B_SIB + 1, to_sib))

    diagonal = (
        lax.broadcasted_iota(jnp.int32, (128, 128), 0)
        == lax.broadcasted_iota(jnp.int32, (128, 128), 1))
    lane = lax.broadcasted_iota(jnp.int32, (1, 128), 1)
    inverse = jnp.exp((lane % 64).astype(F32) * (-2.0 / 128.0 * LOG_BASE))
    position = jnp.sum(
        jnp.where(diagonal, row_lengths[...].astype(F32), 0.0), axis=1, keepdims=True)
    tables = []
    for t in range(2):
        angle = (position + float(t)) * inverse
        tables.append((jnp.cos(angle), jnp.where(lane < 64, -1.0, 1.0) * jnp.sin(angle)))

    for copy in g_y:
        copy.wait_recv()
    own_pages.wait()
    append = [
        pltpu.make_async_copy(
            arrived.at[k], held.at[pl.ds(1024 + 64 * k, 64)], lsem.at[7 + k])
        for k in range(2)
    ]
    for copy in append:
        copy.start()

    b_up[0].wait_recv()
    b_fup = send(o_piece(0, xh * 4 + dn, 0), B_FUP, to_up)
    b_dn[1].wait_recv()
    b_fdn = send(o_piece(0, xh * 4 + up, 1), B_FDN, to_dn)
    a_up, a_dn, a_fup, a_fdn = {}, {}, {}, {}

    def a_send(r):
        for h in (0, 1):
            for k, chip in enumerate((own_chip, partner_chip)):
                first = 45 * (r - 1) + 2 * k
                a_up[r, k, h] = send(o_piece(r, chip, h), A_UP + first + h, to_up)
                a_dn[r, k, 1 - h] = send(o_piece(r, chip, 1 - h), A_DN + first + 1 - h, to_dn)

    def a_forward(r):
        for k, side in enumerate((xh, 1 - xh)):
            a_up[r, k, 0].wait_recv()
            a_fup[r, k] = send(
                o_piece(r, side * 4 + dn, 0), A_FUP + 45 * (r - 1) + k, to_up)
            a_dn[r, k, 1].wait_recv()
            a_fdn[r, k] = send(
                o_piece(r, side * 4 + up, 1), A_FDN + 45 * (r - 1) + k, to_dn)

    def a_near(r):
        for k, side in enumerate((xh, 1 - xh)):
            first = A_SIB + 45 * (r - 1) + 2 + 2 * k
            a_up[r, k, 1].wait_recv()
            a_sib[r].append(send(o_block(r, side * 4 + dn), first, to_sib))
            a_dn[r, k, 0].wait_recv()
            a_sib[r].append(send(o_block(r, side * 4 + up), first + 1, to_sib))

    def a_far(r):
        for k, side in enumerate((xh, 1 - xh)):
            first = A_SIB + 45 * (r - 1) + 6 + 2 * k
            a_fup[r, k].wait_recv()
            a_sib[r].append(send(o_piece(r, side * 4 + opp, 0), first, to_sib))
            a_fdn[r, k].wait_recv()
            a_sib[r].append(send(o_piece(r, side * 4 + opp, 1), first + 1, to_sib))

    a_send(1)

    for copy in p_x:
        copy.wait_recv()
    for t in range(2):
        rows = pl.ds(t * 128, 128)
        cos, sin = tables[t]

        def whole(part, first):
            cols = pl.ds(first, HD)
            return acc[part][0, rows, cols] + precv[part][rows, cols].astype(F32)

        def rotated(value):
            turned = jnp.concatenate([value[:, 64:], value[:, :64]], axis=1)
            return (value * cos + turned * sin).astype(BF16).astype(F32)

        k_new[rows, :] = rotated(whole(0, 0))
        v_new[rows, :] = whole(0, HD).astype(BF16).astype(F32)
        for h in range(4):
            q3[:, t * 8 + h, :] = rotated(whole(0, (h + 2) * HD))
            q3[:, t * 8 + 4 + h, :] = rotated(whole(1, h * HD))
    for copy in append:
        copy.wait()

    b_up[1].wait_recv()
    b_sib.append(send(o_block(0, xh * 4 + dn), B_SIB + 2, to_sib))
    b_x.append(send(o_block(0, xh * 4 + dn), B_X + 1, to_x))
    b_dn[0].wait_recv()
    b_sib.append(send(o_block(0, xh * 4 + up), B_SIB + 3, to_sib))
    b_x.append(send(o_block(0, xh * 4 + up), B_X + 2, to_x))

    scale = 1.0 / HD**0.5
    place = lax.broadcasted_iota(jnp.int32, (16, 128), 1)
    second = lax.broadcasted_iota(jnp.int32, (GROUP * 16, 1), 0) % 16 >= 8

    def attend(i, carry):
        base = i * GROUP
        query = q3[pl.ds(pl.multiple_of(base, GROUP), GROUP)].reshape(GROUP * 16, HD)
        query_low = query.astype(BF16)

        def spread(ref, t):
            value = ref[pl.ds(pl.multiple_of(t * 128 + base, GROUP), GROUP), :]
            return jnp.broadcast_to(
                value[:, None, :], (GROUP, 16, HD)).reshape(GROUP * 16, HD)

        new0 = jnp.sum(query * spread(k_new, 0), axis=1, keepdims=True) * scale
        new1 = jnp.sum(query * spread(k_new, 1), axis=1, keepdims=True) * scale
        new1 = jnp.where(second, new1, -jnp.inf)
        caches = [
            jnp.concatenate([held[table[base + k, j]] for j in range(8)], axis=0)
            for k in range(GROUP)
        ]
        scores = [
            lax.dot_general(
                query_low[k * 16:(k + 1) * 16], caches[k][:, :HD], (((1,), (1,)), ((), ())),
                preferred_element_type=F32)
            for k in range(GROUP)
        ]
        scores = jnp.concatenate([
            jnp.where(place < lengths[base + k], scores[k] * scale, -jnp.inf)
            for k in range(GROUP)], axis=0)
        top = jnp.maximum(jnp.max(scores, axis=1, keepdims=True), jnp.maximum(new0, new1))
        weights = jnp.exp(scores - top)
        weight0 = jnp.exp(new0 - top)
        weight1 = jnp.exp(new1 - top)
        total = jnp.sum(weights, axis=1, keepdims=True) + weight0 + weight1
        weights = weights.astype(BF16)
        numer = jnp.concatenate([
            jnp.dot(weights[k * 16:(k + 1) * 16], caches[k][:, HD:], preferred_element_type=F32)
            for k in range(GROUP)], axis=0)
        numer = numer + weight0.astype(BF16).astype(F32) * spread(v_new, 0)
        numer = numer + weight1.astype(BF16).astype(F32) * spread(v_new, 1)
        q3[pl.ds(pl.multiple_of(base, GROUP), GROUP)] = (numer / total).reshape(GROUP, 16, HD)
        return carry

    lax.fori_loop(0, 128 // GROUP, attend, 0)
    for t in range(2):
        for h in range(8):
            attn[pl.ds(t * 128, 128), pl.ds(h * HD, HD)] = q3[:, t * 8 + h, :].astype(BF16)

    halves = (pl.ds(0, 128), pl.ds(128, 128))

    def z_remote(src, dst, r, chip, h, sem, device):
        return pltpu.make_async_remote_copy(
            src_ref=src, dst_ref=dst, send_sem=z_ssem.at[r, chip, h], recv_sem=sem,
            device_id=device, device_id_type=MESH)

    def far_copy(r, chip, h):
        return z_remote(
            part[r].at[chip, halves[h]], zmid[r].at[h, chip % 2], r, chip, h,
            mid_rsem.at[r, h, chip % 2], at_z(z_up if h else z_dn))

    def near_copy(r, chip, side, h):
        rows = pl.ds(pl.multiple_of(h * 128, 128), 128)
        return z_remote(
            part[r].at[chip, rows], zrecv[r].at[side, chip % 2, rows], r, chip, h,
            z_rsem.at[r, side, chip % 2, h], at_z((z + 3 + 2 * side) % 4))

    def distance(chip):
        return (z - chip // 2 + 4) % 4

    def unit(r, chip):
        for n in range(SPAN[r] // 128):
            cols = pl.ds(n * 256, 256)
            if SPAN[r] == 256:
                weight = wo[r][chip, n]
            else:
                weight = jnp.concatenate([wo[r][chip, 0], wo[r][chip, 1]], axis=1)
            part[r][chip, :, cols] = jnp.dot(
                attn[...], weight, preferred_element_type=F32).astype(BF16)
        d = distance(chip)

        @pl.when(d == 2)
        def _():
            far_copy(r, chip, 0).start()
            far_copy(r, chip, 1).start()

        @pl.when(d % 2 == 1)
        def _():
            side = d // 2
            near_copy(r, chip, side, 1 - side).start()

    def late(r, chip):
        d = distance(chip)

        @pl.when(d % 2 == 1)
        def _():
            side = d // 2
            rows = pl.ds(pl.multiple_of(side * 128, 128), 128)
            landing = zmid[r].at[side, chip % 2]
            pltpu.make_async_copy(landing, landing, mid_rsem.at[r, side, chip % 2]).wait()
            part[r][chip, rows] = (
                part[r][chip, rows].astype(F32) + zmid[r][side, chip % 2].astype(F32)
            ).astype(BF16)
            near_copy(r, chip, side, side).start()

    waiting = []

    def run(r, chip):
        unit(r, chip)
        waiting.append((r, chip))
        if len(waiting) > 5:
            late(*waiting.pop(0))

    b_fup.wait_recv()
    b_x.append(send(o_piece(0, xh * 4 + opp, 0), B_X + 3, to_x))
    b_sib.append(send(o_piece(0, xh * 4 + opp, 0), B_SIB + 4, to_sib))
    b_fdn.wait_recv()
    b_x.append(send(o_piece(0, xh * 4 + opp, 1), B_X + 4, to_x))
    b_sib.append(send(o_piece(0, xh * 4 + opp, 1), B_SIB + 5, to_sib))
    for r in (1, 2):
        a_sib[r][0].wait_recv()
        run(r, own_chip)
    b_sib[0].wait_recv()
    run(0, own_chip)
    a_forward(1)
    a_send(2)
    for r in (1, 2):
        a_sib[r][1].wait_recv()
        run(r, partner_chip)
    b_sib[1].wait_recv()
    run(0, partner_chip)
    b_sib[2].wait_recv()
    run(0, xh * 4 + dn)
    b_sib[3].wait_recv()
    run(0, xh * 4 + up)
    a_near(1)
    b_sib[4].wait_recv()
    b_sib[5].wait_recv()
    run(0, xh * 4 + opp)

    def run_near(r):
        for k, side in enumerate((xh, 1 - xh)):
            a_sib[r][2 + 2 * k].wait_recv()
            run(r, side * 4 + dn)
            a_sib[r][3 + 2 * k].wait_recv()
            run(r, side * 4 + up)

    def run_far(r):
        for k, side in enumerate((xh, 1 - xh)):
            a_sib[r][6 + 2 * k].wait_recv()
            a_sib[r][7 + 2 * k].wait_recv()
            run(r, side * 4 + opp)

    def flush(left):
        while len(waiting) > left:
            late(*waiting.pop(0))

    def z_sum(r, lo):
        total = part[r][z * 2 + lo].astype(F32)
        for side in range(2):
            total = total + zrecv[r][side, lo].astype(F32)
        return total

    def z_wait(r, lo):
        for side in range(2):
            for h in range(2):
                landing = zrecv[r].at[side, lo, halves[h]]
                pltpu.make_async_copy(landing, landing, z_rsem.at[r, side, lo, h]).wait()

    r_x = {}

    def reduce_other(r):
        z_wait(r, 1 - xl)
        xsend[r][...] = z_sum(r, 1 - xl).astype(BF16)
        r_x[r] = send(xsend[r], R_X + r, to_lo, xrecv[r])

    def reduce_own(r):
        z_wait(r, xl)
        r_x[r].wait_recv()
        total = (z_sum(r, xl) + xrecv[r][...].astype(F32)).astype(BF16)
        for core in range(2):
            out[:, pl.ds(core * 512 + FIRST[r], SPAN[r])] = (
                total[:, core * SPAN[r]:(core + 1) * SPAN[r]])

    run_near(1)
    for k, chip in enumerate(((1 - xh) * 4 + dn, (1 - xh) * 4 + up)):
        b_x[1 + k].wait_recv()
        b_sib.append(send(o_block(0, chip), B_SIB + 6 + k, to_sib))
    a_far(1)
    a_forward(2)
    for k, chip in enumerate(((1 - xh) * 4 + dn, (1 - xh) * 4 + up)):
        b_sib[6 + k].wait_recv()
        run(0, chip)
    run_far(1)
    for h in (0, 1):
        b_x[3 + h].wait_recv()
        b_sib.append(send(o_piece(0, (1 - xh) * 4 + opp, h), B_SIB + 8 + h, to_sib))
    a_near(2)
    b_sib[8].wait_recv()
    b_sib[9].wait_recv()
    run(0, (1 - xh) * 4 + opp)
    run_near(2)
    flush(4)
    a_far(2)
    reduce_other(1)
    run_far(2)
    flush(2)
    reduce_other(0)
    flush(0)
    reduce_other(2)
    reduce_own(1)
    reduce_own(0)
    reduce_own(2)

    for copy in sent:
        copy.wait_send()
    for r in range(3):
        for chip in range(8):
            @pl.when(distance(chip) != 0)
            def _():
                for h in range(2):
                    rows = part[r].at[chip, halves[h]]
                    pltpu.make_async_copy(rows, rows, z_ssem.at[r, chip, h]).wait()


def per_device(tokens, q_weight, kv_weight, o_weight, kv_pool, send_list, page_table, lengths):
    rows = tokens.shape[1]
    hbm = pl.BlockSpec(memory_space=pl.ANY)
    vmem = pl.BlockSpec(memory_space=pltpu.VMEM)
    smem = pl.BlockSpec(memory_space=pltpu.SMEM)
    mixed = pl.pallas_call(
        kernel,
        out_shape=jax.ShapeDtypeStruct((256, 1024), BF16),
        in_specs=[hbm] * 5 + [vmem] + [smem] * 3,
        out_specs=vmem,
        scratch_shapes=[
            pltpu.VMEM((4, 1024, WIDTH[0]), BF16),
            pltpu.VMEM((4, 1024, WIDTH[1]), BF16),
            *[pltpu.VMEM((8, 2, 1024, span), BF16) for span in SPAN],
            pltpu.VMEM((2, 256, 4096), BF16),
            pltpu.VMEM((1152, 16, 256), BF16),
            pltpu.VMEM((2, 64, 16, 256), BF16),
            pltpu.VMEM((64, 16, 256), BF16),
            pltpu.VMEM((2, 64, 16, 256), BF16),
            pltpu.VMEM((2, 256, WIDTH[0]), F32),
            pltpu.VMEM((2, 256, WIDTH[1]), F32),
            pltpu.VMEM((256, WIDTH[0]), BF16),
            pltpu.VMEM((256, WIDTH[1]), BF16),
            pltpu.VMEM((256, WIDTH[0]), BF16),
            pltpu.VMEM((256, WIDTH[1]), BF16),
            pltpu.VMEM((128, 16, 128), F32),
            pltpu.VMEM((256, 128), F32),
            pltpu.VMEM((256, 128), F32),
            pltpu.VMEM((256, 1024), BF16),
            *[pltpu.VMEM((8, 256, 2 * span), BF16) for span in SPAN],
            *[pltpu.VMEM((2, 2, 128, 2 * span), BF16) for span in SPAN],
            *[pltpu.VMEM((2, 2, 256, 2 * span), BF16) for span in SPAN],
            *[pltpu.VMEM((256, 2 * span), BF16) for span in SPAN * 2],
            pltpu.SemaphoreType.DMA((N_REMOTE,)),
            pltpu.SemaphoreType.DMA((N_REMOTE,)),
            pltpu.SemaphoreType.DMA((3, 8, 2)),
            pltpu.SemaphoreType.DMA((3, 2, 2)),
            pltpu.SemaphoreType.DMA((3, 2, 2, 2)),
            pltpu.SemaphoreType.DMA((13,)),
        ],
        compiler_params=pltpu.CompilerParams(
            collective_id=0, has_side_effects=True, vmem_limit_bytes=62 * 2**20),
    )(
        tokens.reshape(2 * rows, tokens.shape[2]), q_weight, kv_weight, o_weight, kv_pool,
        lengths.reshape(1, rows), send_list, page_table, lengths,
    )
    return mixed.reshape(2, rows, -1)


def solution(mesh):
    in_specs = (
        P(None, "group", None),
        P("group", "mp"),
        P("group", "mp"),
        P("mp", "group"),
        P("group", None, "mp"),
        P("group", None, None),
        P("group", None),
        P("group"),
    )
    out_specs = P(None, "group", "mp")
    return jax.shard_map(
        per_device, mesh=mesh, in_specs=in_specs, out_specs=out_specs, check_vma=False
    )
```
